32 devices in a mesh: groups: 2 (over x), grid: 4 (over y, core), rep: 4 (over z).
Axes of the slice: x: 2, y: 2, z: 4, core: 2. Of those that a mesh axis runs over, the one named last changes fastest.
Arguments:
- x_vals: bfloat16 [512, 6, 128, 128], P(('groups', 'grid', 'rep')), parts along dimension 0, may hold values from -6 to 6
- x_cols: int32 [512, 6], P('groups'), parts along dimension 0, may hold values from 0 to 255, as said below
- p_cols: int32 [512, 10], P('groups'), parts along dimension 0, may hold values from 0 to 255, as said below
Outputs:
- new_vals: bfloat16 [512, 10, 128, 128], P(('groups', 'grid', 'rep')), parts along dimension 0
The draws below stay inside these ranges and needn't reach their ends.
There are 2 independent parts, one for each index of `groups`. The reference program is written for one: setup_inputs(seed, part) draws one part's arguments, and reference() takes and returns one part's arrays. A program takes and returns all parts, laid end to end along the dimension named above; each array names one. Nothing has to cross between parts.
Inputs may be any that keep to these rules, and one draw needn't show every extreme that they name: `x_cols`: block row i lists 6 different block columns (i + d) mod 256 with -4 <= d <= 4, d = 0 among them, ordered by increasing d. `p_cols`: block row i lists 10 different block columns (i + d) mod 256 with -8 <= d <= 8, d = 0 among them, ordered by increasing d.
All inputs are finite; a program needn't handle non-finite values.
Results may differ from the reference program's by a relative error of at most 0.0013.
Values may be sent and summed in bfloat16 or wider, within the bound.
No kernel may reach another device: no remote copies, remote signals or barrier semaphores. Data moves between devices by JAX's collectives and lax.ppermute only.
A program may use at most 64 MiB of HBM per device.

```python
import jax
import jax.numpy as jnp
from jax import lax

BLK = 128
NNZ = 6
PNZ = 10
BAND = 4
NB = 256


def band_pattern(key, reach_blocks, slot_count):
    offsets = jnp.concatenate([jnp.arange(-reach_blocks, 0, dtype=jnp.int32), jnp.arange(1, reach_blocks + 1, dtype=jnp.int32)])
    scores = jax.random.randint(key, (NB, 2 * reach_blocks), 0, 1048576, dtype=jnp.int32) * (2 * reach_blocks) + jnp.arange(2 * reach_blocks, dtype=jnp.int32)[None, :]
    picked = jnp.argsort(scores, axis=1)[:, :slot_count - 1]
    chosen = jnp.concatenate([jnp.zeros((NB, 1), jnp.int32), offsets[picked]], axis=1)
    chosen = jnp.sort(chosen, axis=1)
    return (jnp.arange(NB, dtype=jnp.int32)[:, None] + chosen) % NB


def draw_x_cols(key, part):
    key = jax.random.fold_in(key, 11)
    return band_pattern(key, BAND, NNZ)


def draw_p_cols(key, part):
    key = jax.random.fold_in(key, 23)
    return band_pattern(key, 2 * BAND, PNZ)


def level_of(stream_key, extent, pieces, low, largest):
    level, own = 1.0, jax.random.fold_in(stream_key, 6)
    for dim, parts in pieces:
        draws = jnp.exp(jax.random.uniform(jax.random.fold_in(own, dim), (parts,), jnp.float32, low / len(pieces), largest / len(pieces)))
        level = level * jnp.repeat(draws, extent[dim] // parts).reshape([-1 if axis == dim else 1 for axis in range(len(extent))])
    return level


def noise(key, shape, spread, limit, split=(), kind=jnp.bfloat16):
    result = spread * jax.random.normal(key, shape, jnp.float32)
    if split:
        result = result * level_of(key, shape, split, -0.22, 0.18)
    return jnp.clip(result, -limit, limit).astype(kind)


def setup_inputs(seed: int = 0, part: int = 0) -> dict:
    streams_of = jax.random.split(jax.random.key(seed), 4)
    part_keys = jax.random.split(jax.random.fold_in(streams_of[3], part), 4)
    x_vals = noise(part_keys[0], (NB, NNZ, BLK, BLK), 1.0, 6.0, ((0, 16),))
    x_cols = draw_x_cols(jax.random.fold_in(jax.random.fold_in(streams_of[3], part), 71), part)
    p_cols = draw_p_cols(jax.random.fold_in(jax.random.fold_in(streams_of[3], part), 71), part)
    return dict(x_vals=x_vals, x_cols=x_cols, p_cols=p_cols)


def reference(x_vals, x_cols, p_cols):
    gram_scale = 1.0 / (4 * NNZ * BLK)

    def gram_block_row(natural_row):
        own_blocks = x_vals[natural_row].astype(jnp.float32)
        neighbour_rows = x_cols[natural_row]
        far_blocks = x_vals[neighbour_rows].astype(jnp.float32)
        products = jnp.einsum("axz,abzy->abxy", own_blocks, far_blocks, preferred_element_type=jnp.float32)
        matches = (x_cols[neighbour_rows][:, :, None] == p_cols[natural_row][None, None, :]).astype(jnp.float32)
        summed = jnp.einsum("abp,abxy->pxy", matches, products, precision=lax.Precision.HIGHEST)
        return (summed * gram_scale).astype(jnp.bfloat16)

    gram = lax.map(gram_block_row, jnp.arange(NB, dtype=jnp.int32))

    def update_block_row(natural_row):
        own_blocks = x_vals[natural_row].astype(jnp.float32)
        neighbour_rows = x_cols[natural_row]
        far_blocks = gram[neighbour_rows].astype(jnp.float32)
        products = jnp.einsum("axz,aczy->acxy", own_blocks, far_blocks, preferred_element_type=jnp.float32)
        matches = (p_cols[neighbour_rows][:, :, None] == p_cols[natural_row][None, None, :]).astype(jnp.float32)
        carried = jnp.einsum("acp,acxy->pxy", matches, products, precision=lax.Precision.HIGHEST)
        present = (x_cols[natural_row][:, None] == p_cols[natural_row][None, :]).astype(jnp.float32)
        kept = jnp.einsum("bp,bxy->pxy", present, own_blocks, precision=lax.Precision.HIGHEST)
        return (1.5 * kept - 0.5 * carried).astype(jnp.bfloat16)

    return lax.map(update_block_row, jnp.arange(NB, dtype=jnp.int32))
```

```python
from functools import partial

import jax
import jax.numpy as jnp
from jax import lax
from jax.experimental import pallas as pl
from jax.experimental.pallas import tpu as pltpu
from jax.sharding import PartitionSpec as P

BAND = 4
REACH = 2 * BAND
AXES = ("grid", "rep")
MIB = 1024 * 1024


def slot_tables(cols, first_row, row_count, reach, width):
    total, slots = cols.shape
    natural = jnp.arange(total, dtype=jnp.int32)[:, None]
    offsets = (cols - natural + reach) % total - reach
    wrapped = jnp.concatenate([offsets[-REACH:], offsets, offsets[:REACH]], axis=0)
    rows = row_count + 2 * REACH
    local = lax.dynamic_slice_in_dim(wrapped, first_row, rows, axis=0)
    zero = rows * slots
    number = jnp.arange(zero, dtype=jnp.int32).reshape(rows, slots, 1) - zero
    place = jnp.arange(32, dtype=jnp.int32) - width
    table = zero + jnp.sum(jnp.where(local[:, :, None] == place, number, 0), axis=1)
    return local, table.astype(jnp.int32)


def row_product(left, right, right_index, left_blocks, slots, wanted):
    own = jnp.concatenate([left[left_blocks[s]] for s in slots], axis=1)
    sums = []
    for p in range(0, wanted, 2):
        columns = [
            jnp.concatenate([right[right_index(s, q)] for s in slots], axis=0)
            for q in (p, p + 1)
        ]
        sums.append(
            jnp.dot(own, jnp.concatenate(columns, axis=1), preferred_element_type=jnp.float32)
        )
    return sums


def gram_row(r, dx, dp, tx, pool, gram, scale):
    nnz, pnz = dx.shape[1], dp.shape[1]
    shift = [dx[r, s] for s in range(nnz)]
    want = [dp[r, p] + 3 * BAND for p in range(pnz)]
    sums = row_product(
        pool, pool, lambda s, p: tx[r + shift[s], want[p] - shift[s]],
        [r * nnz + s for s in range(nnz)], range(nnz), pnz,
    )
    for q, pair in enumerate(sums):
        scaled = (pair * scale).astype(jnp.bfloat16)
        size = scaled.shape[0]
        gram[r * pnz + 2 * q] = scaled[:, :size]
        gram[r * pnz + 2 * q + 1] = scaled[:, size:]


def update_sums(r, slots, dx, dp, tg, pool, gram):
    nnz, pnz = dx.shape[1], dp.shape[1]
    shift = {s: dx[r, s] for s in slots}
    want = [dp[r, p] + 3 * BAND for p in range(pnz)]
    return row_product(
        pool, gram, lambda s, p: tg[r + shift[s], want[p] - shift[s]],
        {s: r * nnz + s for s in slots}, slots, pnz,
    )


def first_kernel(scale, dx, dp, tx, tg, x, low, high, out, part, pool, gram, done, sems):
    nnz, pnz = dx.shape[1], dp.shape[1]
    own = x.shape[0]
    near = low.shape[0]
    rows = own // nnz
    start = REACH * nnz
    copies = [
        pltpu.make_async_copy(x, pool.at[pl.ds(start, own)], sems.at[0]),
        pltpu.make_async_copy(low, pool.at[pl.ds(start - near, near)], sems.at[1]),
        pltpu.make_async_copy(high, pool.at[pl.ds(start + own, near)], sems.at[2]),
    ]
    for copy in copies:
        copy.start()
    pool[pool.shape[0] - 1] = jnp.zeros(pool.shape[1:], pool.dtype)
    gram[gram.shape[0] - 1] = jnp.zeros(gram.shape[1:], gram.dtype)
    for copy in copies:
        copy.wait()

    @pl.loop(REACH, REACH + rows)
    def _(r):
        gram_row(r, dx, dp, tx, pool, gram, scale)

    def update(r, store):
        sums = update_sums(r, range(nnz), dx, dp, tg, pool, gram)
        for p in range(pnz):
            size = pool.shape[1]
            half = sums[p // 2][:, (p % 2) * size:(p % 2 + 1) * size]
            kept = pool[tx[r, dp[r, p] + 3 * BAND]].astype(jnp.float32)
            store(p, 1.5 * kept - 0.5 * half)

    @pl.loop(BAND, rows - BAND)
    def _(i):
        def store(p, value):
            done[(i - BAND) * pnz + p] = value.astype(done.dtype)

        update(REACH + i, store)

    copy = pltpu.make_async_copy(
        done, out.at[pl.ds(BAND * pnz, (rows - 2 * BAND) * pnz)], sems.at[3]
    )
    copy.start()

    @pl.loop(0, 2 * BAND)
    def _(e):
        def store(p, value):
            part[e * pnz + p] = value

        update(REACH + jnp.where(e < BAND, e, rows - 2 * BAND + e), store)

    copy.wait()


def second_kernel(
    scale, dx, dp, tx, tg, x, low, high, far_low, far_high, part, unused, out, pool, gram, sums, done, sems
):
    nnz, pnz = dx.shape[1], dp.shape[1]
    own = x.shape[0]
    near = low.shape[0]
    rows = own // nnz
    start = REACH * nnz
    moves = [
        (x.at[pl.ds(0, near)], start),
        (x.at[pl.ds(own - near, near)], start + own - near),
        (low, start - near),
        (high, start + own),
        (far_low, start - 2 * near),
        (far_high, start + own + near),
    ]
    copies = [
        pltpu.make_async_copy(source, pool.at[pl.ds(place, near)], sems.at[n])
        for n, (source, place) in enumerate(moves)
    ]
    for copy in copies:
        copy.start()
    late = pltpu.make_async_copy(part, sums, sems.at[len(moves)])
    late.start()
    pool[pool.shape[0] - 1] = jnp.zeros(pool.shape[1:], pool.dtype)
    gram[gram.shape[0] - 1] = jnp.zeros(gram.shape[1:], gram.dtype)
    for copy in copies:
        copy.wait()

    @pl.loop(0, 2 * BAND)
    def _(e):
        r = jnp.where(e < BAND, REACH - BAND + e, REACH + rows - BAND + e)
        gram_row(r, dx, dp, tx, pool, gram, scale)

    late.wait()
    outgoing = []
    for e in range(2 * BAND):
        if e < BAND:
            i, slots = e, range(0, BAND - e)
        else:
            i, slots = rows - 2 * BAND + e, range(nnz - 1 - (e - BAND), nnz)
        found = update_sums(REACH + i, slots, dx, dp, tg, pool, gram)
        for p in range(pnz):
            size = pool.shape[1]
            half = found[p // 2][:, (p % 2) * size:(p % 2 + 1) * size]
            done[e * pnz + p] = (sums[e * pnz + p] - 0.5 * half).astype(done.dtype)
        copy = pltpu.make_async_copy(
            done.at[pl.ds(e * pnz, pnz)], out.at[pl.ds(i * pnz, pnz)], sems.at[len(moves) + 1 + e]
        )
        copy.start()
        outgoing.append(copy)
    for copy in outgoing:
        copy.wait()


def body(x_vals, x_cols, p_cols):
    rows, nnz, size, _ = x_vals.shape
    pnz = p_cols.shape[1]
    count = lax.axis_size(AXES)
    first_row = lax.axis_index(AXES) * rows
    scale = 1.0 / (4 * nnz * size)
    padded = rows + 2 * REACH
    forward = [(i, (i + 1) % count) for i in range(count)]
    backward = [(target, source) for source, target in forward]

    x = x_vals.reshape(rows * nnz, size, size)
    near = BAND * nnz
    low = lax.ppermute(x[rows * nnz - near:], AXES, forward)
    high = lax.ppermute(x[:near], AXES, backward)
    far_low = lax.ppermute(x[rows * nnz - 2 * near:rows * nnz - near], AXES, forward)
    far_high = lax.ppermute(x[near:2 * near], AXES, backward)

    dx, tx = slot_tables(x_cols, first_row, rows, BAND, 3 * BAND)
    dp, tg = slot_tables(p_cols, first_row, rows, REACH, 3 * BAND)
    row = jnp.arange(padded)[:, None]
    mine = (row >= REACH) & (row < REACH + rows)
    tg_own = jnp.where(mine, tg, padded * pnz)
    tg_far = jnp.where(mine, padded * pnz, tg)

    smem = pl.BlockSpec(memory_space=pltpu.SMEM)
    hbm = pl.BlockSpec(memory_space=pl.ANY)
    vmem = pl.BlockSpec(memory_space=pltpu.VMEM)
    block = (size, size)
    pool = pltpu.VMEM((padded * nnz + 1,) + block, jnp.bfloat16)
    gram = pltpu.VMEM((padded * pnz + 1,) + block, jnp.bfloat16)
    edge = 2 * BAND * pnz
    out_type = jax.ShapeDtypeStruct((rows * pnz,) + block, jnp.bfloat16)
    product = 2 * size ** 3
    out, part = pl.pallas_call(
        partial(first_kernel, scale),
        out_shape=(out_type, jax.ShapeDtypeStruct((edge,) + block, jnp.float32)),
        in_specs=[smem] * 4 + [hbm] * 3,
        out_specs=(hbm, vmem),
        scratch_shapes=[
            pool,
            gram,
            pltpu.VMEM(((rows - 2 * BAND) * pnz,) + block, jnp.bfloat16),
            pltpu.SemaphoreType.DMA((4,)),
        ],
        compiler_params=pltpu.CompilerParams(vmem_limit_bytes=48 * MIB),
        cost_estimate=pl.CostEstimate(
            flops=rows * 2 * nnz * pnz * product, bytes_accessed=16 * MIB, transcendentals=0
        ),
    )(dx, dp, tx, tg_own, x, low, high)
    out = pl.pallas_call(
        partial(second_kernel, scale),
        out_shape=out_type,
        in_specs=[smem] * 4 + [hbm] * 7,
        out_specs=hbm,
        input_output_aliases={10: 0},
        scratch_shapes=[
            pool,
            gram,
            pltpu.VMEM((edge,) + block, jnp.float32),
            pltpu.VMEM((edge,) + block, jnp.bfloat16),
            pltpu.SemaphoreType.DMA((7 + 2 * BAND,)),
        ],
        compiler_params=pltpu.CompilerParams(vmem_limit_bytes=48 * MIB),
        cost_estimate=pl.CostEstimate(
            flops=2 * BAND * 2 * nnz * pnz * product, bytes_accessed=16 * MIB, transcendentals=0
        ),
    )(dx, dp, tx, tg_far, x, low, high, far_low, far_high, part, out)
    return out.reshape(rows, pnz, size, size)


def solution(mesh):
    return jax.shard_map(
        body,
        mesh=mesh,
        in_specs=(
            P(("groups", "grid", "rep"), None, None, None),
            P("groups", None),
            P("groups", None),
        ),
        out_specs=P(("groups", "grid", "rep"), None, None, None),
        check_vma=False,
    )
```

```python
from functools import partial

import jax
import jax.numpy as jnp
from jax import lax
from jax.experimental import pallas as pl
from jax.experimental.pallas import tpu as pltpu
from jax.sharding import PartitionSpec as P

BAND = 4
REACH = 2 * BAND
CENTRE = 3 * BAND
AXES = ("grid", "rep")
MIB = 1024 * 1024
FIRST = 12
STEPS = 8
BIG = 60
TO_X, TO_GRAM, TO_FAR, TO_HALO = 0, 32, 64, 96
LANES = 128
SPARE = 25
SENT = TO_HALO + SPARE


def shift_lane(s):
    return TO_X + SPARE + s


def want_lane(p):
    free = 32 - SPARE
    return (TO_GRAM + SPARE + p) if p < free else (TO_FAR + SPARE + p - free)


def bit_count(v):
    v = v - ((v >> 1) & 0x55555555)
    v = (v & 0x33333333) + ((v >> 2) & 0x33333333)
    v = (v + (v >> 4)) & 0x0F0F0F0F
    return (v + (v >> 8) + (v >> 16)) & 0x3F


def plan_kernel(dims, me, x_cols, p_cols, ints, largest):
    rows, nnz, pnz = dims
    total = x_cols.shape[1]
    padded = rows + 2 * REACH
    most = BAND * nnz
    edge = 2 * BAND * pnz
    lane = lax.broadcasted_iota(jnp.int32, (8, total), 1)
    sub = lax.broadcasted_iota(jnp.int32, (8, total), 0)

    def offsets(ref, count, reach):
        index = lax.broadcasted_iota(jnp.int32, (count, total), 1)
        off = ref[...] - index
        off = jnp.where(off < -reach, off + total, off)
        return jnp.where(off > reach, off - total, off)

    x_off, p_off = offsets(x_cols, nnz, BAND), offsets(p_cols, pnz, REACH)

    def masks(off, reach, axis):
        one = jnp.int32(1)
        parts = [
            lax.slice_in_dim(off, s, s + 1, axis=axis) for s in range(off.shape[axis])
        ]
        return sum(one << (part + reach) for part in parts)

    x_mask = jnp.broadcast_to(masks(x_off, BAND, 0), (8, total))
    p_mask = jnp.broadcast_to(masks(p_off, REACH, 0), (8, total))

    def framed(mask, t, left):
        return pltpu.roll(mask, (REACH - t) % total, 1) << left

    x_frame = [framed(x_mask, t, t) for t in range(2 * REACH)]
    p_frame = {t: framed(p_mask, t, t - BAND) for t in range(BAND, 3 * BAND)}

    def holds(mask, t):
        return -((mask >> (t + BAND)) & 1)

    def side(i, k, far):
        wanted = {}
        for tk in range(k, k + BAND):
            found = jnp.zeros_like(x_mask)
            for ti in range(i, i + BAND):
                found = found | (p_frame[ti] & holds(x_frame[ti], tk))
            wanted[tk] = found & p_frame[tk]
        used = []
        for tf in range(far, far + BAND):
            found = jnp.zeros_like(x_mask)
            for tk in range(k, k + BAND):
                found = found | (wanted[tk] & holds(x_frame[tk], tf))
            used.append((found & x_frame[tf]) >> tf)
        return used

    up, down = side(REACH, BAND, 0), side(BAND, REACH, 3 * BAND)
    needed = jnp.maximum(sum(map(bit_count, up)), sum(map(bit_count, down)))
    needed = jnp.where(lane % rows == 0, needed, 0)
    largest[...] = jnp.broadcast_to(jnp.max(needed, axis=(0, 1), keepdims=True), largest.shape)

    used = jnp.zeros_like(x_mask)
    for q, mask in enumerate(up + down):
        used = jnp.where(sub == q, mask, used)
    here = me[0] * rows
    above = jnp.where(here + rows == total, 0, here + rows)
    at_here = jnp.sum(jnp.where(lane == here, used, 0), axis=1, keepdims=True)
    at_above = jnp.sum(jnp.where(lane == above, used, 0), axis=1, keepdims=True)

    def one(column, q):
        return lax.slice_in_dim(column, q, q + 1, axis=0)

    row = lax.broadcasted_iota(jnp.int32, (padded, 1), 0)
    wide_lane = lax.broadcasted_iota(jnp.int32, (padded, total), 1)
    wide_row = lax.broadcasted_iota(jnp.int32, (padded, total), 0)
    source = here - REACH + wide_row
    source = jnp.where(source < 0, source + total, source)
    source = jnp.where(source >= total, source - total, source)
    pick = (wide_lane == source).astype(jnp.float32)

    def picked(off):
        return lax.dot_general(
            pick, off.astype(jnp.float32), (((1,), (1,)), ((), ())),
            preferred_element_type=jnp.float32,
        ).astype(jnp.int32)

    dx, dp = picked(x_off), picked(p_off)
    x_row, p_row = masks(dx, BAND, 1), masks(dp, REACH, 1)
    far_row = jnp.zeros((padded, 1), jnp.int32)
    far_base = jnp.zeros((padded, 1), jnp.int32)
    sent = jnp.zeros((padded, 1), jnp.int32)
    base_low = jnp.zeros((1, 1), jnp.int32)
    base_high = jnp.full((1, 1), most, jnp.int32)
    for q in range(BAND):
        t = BAND - 1 - q
        low, high = one(at_here, t), one(at_above, BAND + q)
        place = padded - BAND + q
        far_row = jnp.where(row == t, low, jnp.where(row == place, high, far_row))
        far_base = jnp.where(row == t, base_low, jnp.where(row == place, base_high, far_base))
        base_low = base_low + bit_count(low)
        base_high = base_high + bit_count(high)
        sent = jnp.where(row == rows + t, one(at_above, t), sent)
        sent = jnp.where(row == REACH + BAND + q, one(at_here, BAND + q), sent)

    column = lax.broadcasted_iota(jnp.int32, (padded, LANES), 1)
    place = column & 31

    def looked_up(mask, reach):
        at = place - (CENTRE - reach)
        inside = (at >= 0) & (at <= 2 * reach)
        at = jnp.where(inside, at, 0)
        return inside & (((mask >> at) & 1) == 1), bit_count(mask & ((1 << at) - 1))

    close = (row >= BAND) & (row < padded - BAND)
    own = (row >= REACH) & (row < REACH + rows)
    x_hit, x_slot = looked_up(x_row, BAND)
    p_hit, p_slot = looked_up(p_row, REACH)
    far_hit, far_rank = looked_up(far_row, BAND)
    halo = jnp.where(row < REACH, row - BAND, row - rows - REACH + BAND) * pnz
    table = jnp.where(x_hit & close, row * nnz + x_slot, padded * nnz)
    to_gram = jnp.where(p_hit & own, (row - REACH) * pnz + p_slot, rows * pnz)
    to_far = jnp.where(far_hit, far_base + far_rank, 2 * most)
    to_halo = jnp.where(p_hit & close & ~own, halo + p_slot, edge)
    table = jnp.where(column >= TO_GRAM, to_gram, table)
    table = jnp.where(column >= TO_FAR, to_far, table)
    table = jnp.where(column >= TO_HALO, to_halo, table)
    for s in range(nnz):
        table = jnp.where(column == shift_lane(s), lax.slice_in_dim(dx, s, s + 1, axis=1), table)
    for p in range(pnz):
        table = jnp.where(column == want_lane(p), lax.slice_in_dim(dp, p, p + 1, axis=1), table)
    ints[...] = jnp.where(column == SENT, sent, table)


def products(dims, ints, r, slots, table, left, right, base=0):
    _, nnz, pnz = dims
    shift = {s: ints[r, shift_lane(s)] for s in slots}
    want = [ints[r, want_lane(p)] + CENTRE for p in range(pnz)]
    own = jnp.concatenate([left[r * nnz + s - base] for s in slots], axis=1)
    size = left.shape[1]
    blocks = []
    for p in range(0, pnz, 2):
        columns = [
            jnp.concatenate(
                [right[ints[r + shift[s], table + want[q] - shift[s]]] for s in slots], axis=0
            )
            for q in (p, p + 1)
        ]
        pair = jnp.dot(
            own, jnp.concatenate(columns, axis=1), preferred_element_type=jnp.float32
        )
        blocks += [pair[:, :size], pair[:, size:]]
    return blocks


def clear(ref):
    ref[ref.shape[0] - 1] = jnp.zeros(ref.shape[1:], ref.dtype)


def begin(sems, moves):
    copies = []
    for n, (source, target, place) in enumerate(moves):
        copy = pltpu.make_async_copy(
            source, target.at[pl.ds(place, source.shape[0])], sems.at[n]
        )
        copy.start()
        copies.append(copy)
    return copies


def finish(copies):
    for copy in copies:
        copy.wait()


def gather(dims, ints, pool, outs, picks, sem):
    rows, nnz, _ = dims
    copies = []
    for side, arrays in enumerate(outs):
        for n in range(BAND * nnz):
            picks[side, n] = REACH * nnz
        count = jnp.int32(0)
        for q in range(BAND):
            r = REACH + rows - BAND - 1 - q if side == 0 else REACH + BAND + q
            for s in range(nnz):
                picks[side, count] = r * nnz + s
                count = count + ((ints[r, SENT] >> (ints[r, shift_lane(s)] + BAND)) & 1)
        n = 0
        for out in arrays:
            for place in range(out.shape[0]):
                copy = pltpu.make_async_copy(
                    pool.at[pl.ds(picks[side, n], 1)], out.at[pl.ds(place, 1)], sem.at[side, n]
                )
                copy.start()
                copies.append(copy)
                n += 1
    return copies


def inner_kernel(
    dims, scale, ints, x, out, up, down, up_rest, down_rest, pool, gram, picks, sems, pick_sems
):
    rows, nnz, pnz = dims
    copies = begin(sems, [(x, pool, REACH * nnz)])
    clear(pool)
    finish(copies)
    outs = ((up, up_rest), (down, down_rest))
    listed = gather(dims, ints, pool, outs, picks, pick_sems)

    @pl.loop(0, rows - 2 * BAND)
    def _(i):
        r = REACH + BAND + i
        for p, block in enumerate(products(dims, ints, r, range(nnz), TO_X, pool, pool)):
            gram[i * pnz + p] = (block * scale).astype(gram.dtype)

    finish(begin(sems, [(gram, out, 0)]) + listed)


def near_kernel(
    dims, scale, ints, x, low, high, inner, out, part, gram_part, pool, gram, done, kept_sums,
    near_sums, sems
):
    rows, nnz, pnz = dims
    start = REACH * nnz
    edge = BAND * pnz
    own, near = x.shape[0], low.shape[0]
    half = own // 2
    copies = begin(sems, [
        (low, pool, start - near), (x.at[pl.ds(0, half)], pool, start),
        (high, pool, start + own), (x.at[pl.ds(half, half)], pool, start + half),
        (inner, gram, edge),
    ])
    clear(pool)
    clear(gram)

    def edge_grams(first_row, halo_row, place):
        @pl.loop(0, BAND)
        def _(e):
            i = first_row + e
            blocks = products(dims, ints, REACH + i, range(nnz), TO_X, pool, pool)
            for p, block in enumerate(blocks):
                gram[i * pnz + p] = (block * scale).astype(gram.dtype)

        @pl.loop(0, BAND)
        def _(e):
            r = REACH + halo_row + e
            blocks = products(dims, ints, r, range(nnz), TO_X, pool, pool)
            for p, block in enumerate(blocks):
                near_sums[(place + e) * pnz + p] = block

    finish(copies[:2])
    edge_grams(0, -BAND, 0)
    finish(copies[2:4])
    edge_grams(rows - BAND, rows, BAND)
    finish(copies[4:])
    first = begin(sems.at[pl.ds(0, 1)], [(near_sums, gram_part, 0)])

    def update(r, store):
        blocks = products(dims, ints, r, range(nnz), TO_GRAM, pool, gram)
        for p, block in enumerate(blocks):
            kept = pool[ints[r, TO_X + ints[r, want_lane(p)] + CENTRE]].astype(jnp.float32)
            store(p, 1.5 * kept - 0.5 * block)

    @pl.loop(0, 2 * BAND)
    def _(e):
        def store(p, value):
            kept_sums[e * pnz + p] = value

        update(REACH + jnp.where(e < BAND, e, rows - 2 * BAND + e), store)

    second = begin(sems.at[pl.ds(1, 1)], [(kept_sums, part, 0)])

    @pl.loop(BAND, rows - BAND)
    def _(i):
        def store(p, value):
            done[(i - BAND) * pnz + p] = value.astype(done.dtype)

        update(REACH + i, store)

    third = begin(sems.at[pl.ds(2, 1)], [(done, out, edge)])
    finish(first + second + third)


def far_kernel(
    dims, scale, ints, x, low, high, far_low, far_high, more, part, gram_part, unused, out, pool, far, gram, near_sums, kept_sums, done, sems
):
    rows, nnz, pnz = dims
    near = low.shape[0]
    own = x.shape[0]
    start = BAND * nnz
    edge = BAND * pnz
    first = far_low.shape[0]
    extra = more.shape[0] // 2
    moves = [
        (more.at[pl.ds(0, extra)], far, first),
        (more.at[pl.ds(extra, extra)], far, 2 * first + extra),
        (far_low, far, 0),
        (far_high, far, first + extra),
        (low, pool, start - near),
        (high, pool, start + own),
        (x.at[pl.ds(0, near)], pool, start),
        (x.at[pl.ds(own - near, near)], pool, start + own - near),
    ]
    copies = begin(sems, moves)
    used = len(moves) + 4
    late = begin(sems.at[pl.ds(len(moves), 4)], [
        (half.at[pl.ds(e, edge)], target, e)
        for half, target in ((gram_part, near_sums), (part, kept_sums))
        for e in (0, edge)
    ])
    clear(far)
    clear(gram)
    finish(copies)
    offset = (REACH - BAND) * nnz

    for e in range(2 * BAND):
        if e % BAND == 0:
            late[e // BAND].wait()
        if e < BAND:
            r, slots = REACH - BAND + e, range(0, BAND - e)
        else:
            r, slots = REACH + rows - BAND + e, range(nnz - 1 - (e - BAND), nnz)
        blocks = products(dims, ints, r, slots, TO_FAR, pool, far, offset)
        for p, block in enumerate(blocks):
            n = e * pnz + p
            gram[n] = ((near_sums[n] + block) * scale).astype(gram.dtype)

    outgoing = []
    for e in range(2 * BAND):
        if e % BAND == 0:
            late[2 + e // BAND].wait()
        if e < BAND:
            i, slots = e, range(0, BAND - e)
        else:
            i, slots = rows - 2 * BAND + e, range(nnz - 1 - (e - BAND), nnz)
        blocks = products(dims, ints, REACH + i, slots, TO_HALO, pool, gram, offset)
        for p, block in enumerate(blocks):
            n = e * pnz + p
            done[n] = (kept_sums[n] - 0.5 * block).astype(done.dtype)
        outgoing += begin(
            sems.at[pl.ds(used + e, 1)], [(done.at[pl.ds(e * pnz, pnz)], out, i * pnz)]
        )
    finish(outgoing)


def body(x_vals, x_cols, p_cols):
    rows, nnz, size, _ = x_vals.shape
    pnz = p_cols.shape[1]
    count = lax.axis_size(AXES)
    me = lax.axis_index(AXES)
    first_row = me * rows
    scale = 1.0 / (4 * nnz * size)
    padded = rows + 2 * REACH
    forward = [(i, (i + 1) % count) for i in range(count)]
    backward = [(target, source) for source, target in forward]
    near = BAND * nnz
    edge = 2 * BAND * pnz
    most = near
    first = min(FIRST, most)
    product = 2 * size ** 3
    block = (size, size)

    smem = pl.BlockSpec(memory_space=pltpu.SMEM)
    hbm = pl.BlockSpec(memory_space=pl.ANY)
    vmem = pl.BlockSpec(memory_space=pltpu.VMEM)

    def shaped(blocks, kind=jnp.bfloat16):
        return jax.ShapeDtypeStruct((blocks,) + block, kind)

    def scratch(blocks, kind=jnp.bfloat16):
        return pltpu.VMEM((blocks,) + block, kind)

    def settings(mib):
        return pltpu.CompilerParams(vmem_limit_bytes=mib * MIB)

    def cost(products_made, blocks_moved):
        return pl.CostEstimate(
            flops=products_made * product, bytes_accessed=blocks_moved * 2 * size * size,
            transcendentals=0,
        )

    x = x_vals.reshape(rows * nnz, size, size)
    low = lax.ppermute(x[rows * nnz - near:], AXES, forward)
    high = lax.ppermute(x[:near], AXES, backward)

    dims = (rows, nnz, pnz)
    ints, largest = pl.pallas_call(
        partial(plan_kernel, dims),
        out_shape=(
            jax.ShapeDtypeStruct((padded, LANES), jnp.int32),
            jax.ShapeDtypeStruct((8, LANES), jnp.int32),
        ),
        in_specs=[smem, vmem, vmem],
        out_specs=(vmem, vmem),
        compiler_params=settings(BIG),
    )(me.astype(jnp.int32).reshape(1), x_cols.T, p_cols.T)
    largest = lax.pmax(largest[0, 0], "groups")

    lists = pltpu.SMEM((2, 32), jnp.int32)
    remaining = most - first
    inner, up, down, up_rest, down_rest = pl.pallas_call(
        partial(inner_kernel, dims, scale),
        out_shape=[
            shaped((rows - 2 * BAND) * pnz), shaped(first), shaped(first), shaped(remaining),
            shaped(remaining),
        ],
        in_specs=[smem, hbm],
        out_specs=[hbm] * 5,
        scratch_shapes=[
            scratch(padded * nnz + 1),
            scratch((rows - 2 * BAND) * pnz),
            lists,
            pltpu.SemaphoreType.DMA((1,)),
            pltpu.SemaphoreType.DMA((2, most)),
        ],
        compiler_params=settings(BIG),
        cost_estimate=cost((rows - 2 * BAND) * nnz * pnz, 200),
    )(ints, x)
    far_low = lax.ppermute(up, AXES, forward)
    far_high = lax.ppermute(down, AXES, backward)

    def near_step(low, high, inner):
        return pl.pallas_call(
            partial(near_kernel, dims, scale),
            out_shape=[
                shaped(rows * pnz), shaped(edge, jnp.float32), shaped(edge, jnp.float32)
            ],
            in_specs=[smem] + [hbm] * 4,
            out_specs=[hbm] * 3,
            scratch_shapes=[
                scratch(padded * nnz + 1),
                scratch(rows * pnz + 1),
                scratch((rows - 2 * BAND) * pnz),
                scratch(edge, jnp.float32),
                scratch(edge, jnp.float32),
                pltpu.SemaphoreType.DMA((5,)),
            ],
            compiler_params=settings(BIG),
            cost_estimate=cost((4 * BAND + rows) * nnz * pnz, 900),
        )(ints, x, low, high, inner)

    def step(many, up, down, low, high, inner):
        blank = jnp.zeros((remaining - many,) + block, jnp.bfloat16)
        more = [blank, blank]
        if many:
            more_low = lax.ppermute(up[:many], AXES, forward)
            more_high = lax.ppermute(down[:many], AXES, backward)
            more = [more_low, blank, more_high, blank]
        return *near_step(low, high, inner), jnp.concatenate(more)

    sizes = [n for n in range(remaining) if n <= STEPS] + [remaining]
    out, part, gram_part, more = lax.switch(
        sum((largest > first + n).astype(jnp.int32) for n in sizes[:-1]),
        [partial(step, many) for many in sizes], up_rest, down_rest, low, high, inner,
    )

    operands = [
        ints, x, low, high, far_low, far_high, more, part, gram_part, out
    ]
    out = pl.pallas_call(
        partial(far_kernel, dims, scale),
        out_shape=shaped(rows * pnz),
        in_specs=[smem] + [hbm] * (len(operands) - 1),
        out_specs=hbm,
        input_output_aliases={len(operands) - 1: 0},
        scratch_shapes=[
            scratch((rows + 2 * BAND) * nnz),
            scratch(2 * most + 1),
            scratch(edge + 1),
            scratch(edge, jnp.float32),
            scratch(edge, jnp.float32),
            scratch(edge),
            pltpu.SemaphoreType.DMA((12 + 2 * BAND,)),
        ],
        compiler_params=settings(BIG),
        cost_estimate=cost(2 * BAND * nnz * pnz, 600),
    )(*operands)
    return out.reshape(rows, pnz, size, size)


def solution(mesh):
    return jax.shard_map(
        body,
        mesh=mesh,
        in_specs=(
            P(("groups", "grid", "rep"), None, None, None),
            P("groups", None),
            P("groups", None),
        ),
        out_specs=P(("groups", "grid", "rep"), None, None, None),
        check_vma=False,
    )
```

```python
from functools import partial

import jax
import jax.numpy as jnp
from jax import lax
from jax.experimental import pallas as pl
from jax.experimental.pallas import tpu as pltpu
from jax.sharding import PartitionSpec as P

BAND = 4
REACH = 2 * BAND
CENTRE = 3 * BAND
AXES = ("grid", "rep")
MIB = 1024 * 1024
FIRST = 16
BIG = 60
TO_X, TO_GRAM, TO_FAR, TO_HALO = 0, 32, 64, 96
LANES = 128
SPARE = 25
SENT = TO_HALO + SPARE


def shift_lane(s):
    return TO_X + SPARE + s


def want_lane(p):
    free = 32 - SPARE
    return (TO_GRAM + SPARE + p) if p < free else (TO_FAR + SPARE + p - free)


def bit_count(v):
    v = v - ((v >> 1) & 0x55555555)
    v = (v & 0x33333333) + ((v >> 2) & 0x33333333)
    v = (v + (v >> 4)) & 0x0F0F0F0F
    return (v + (v >> 8) + (v >> 16)) & 0x3F


def plan_kernel(dims, me, x_cols, p_cols, ints, largest):
    rows, nnz, pnz = dims
    total = x_cols.shape[1]
    padded = rows + 2 * REACH
    most = BAND * nnz
    edge = 2 * BAND * pnz
    lane = lax.broadcasted_iota(jnp.int32, (8, total), 1)
    sub = lax.broadcasted_iota(jnp.int32, (8, total), 0)

    def offsets(ref, count, reach):
        index = lax.broadcasted_iota(jnp.int32, (count, total), 1)
        off = ref[...] - index
        off = jnp.where(off < -reach, off + total, off)
        return jnp.where(off > reach, off - total, off)

    x_off, p_off = offsets(x_cols, nnz, BAND), offsets(p_cols, pnz, REACH)

    def masks(off, reach, axis):
        one = jnp.int32(1)
        parts = [
            lax.slice_in_dim(off, s, s + 1, axis=axis) for s in range(off.shape[axis])
        ]
        return sum(one << (part + reach) for part in parts)

    x_mask = jnp.broadcast_to(masks(x_off, BAND, 0), (8, total))
    p_mask = jnp.broadcast_to(masks(p_off, REACH, 0), (8, total))

    def framed(mask, t, left):
        return pltpu.roll(mask, (REACH - t) % total, 1) << left

    x_frame = [framed(x_mask, t, t) for t in range(2 * REACH)]
    p_frame = {t: framed(p_mask, t, t - BAND) for t in range(BAND, 3 * BAND)}

    def holds(mask, t):
        return -((mask >> (t + BAND)) & 1)

    def side(i, k, far):
        wanted = {}
        for tk in range(k, k + BAND):
            found = jnp.zeros_like(x_mask)
            for ti in range(i, i + BAND):
                found = found | (p_frame[ti] & holds(x_frame[ti], tk))
            wanted[tk] = found & p_frame[tk]
        used = []
        for tf in range(far, far + BAND):
            found = jnp.zeros_like(x_mask)
            for tk in range(k, k + BAND):
                found = found | (wanted[tk] & holds(x_frame[tk], tf))
            used.append((found & x_frame[tf]) >> tf)
        return used

    up, down = side(REACH, BAND, 0), side(BAND, REACH, 3 * BAND)
    needed = jnp.maximum(sum(map(bit_count, up)), sum(map(bit_count, down)))
    needed = jnp.where(lane % rows == 0, needed, 0)
    largest[...] = jnp.broadcast_to(jnp.max(needed, axis=(0, 1), keepdims=True), largest.shape)

    used = jnp.zeros_like(x_mask)
    for q, mask in enumerate(up + down):
        used = jnp.where(sub == q, mask, used)
    here = me[0] * rows
    above = jnp.where(here + rows == total, 0, here + rows)
    at_here = jnp.sum(jnp.where(lane == here, used, 0), axis=1, keepdims=True)
    at_above = jnp.sum(jnp.where(lane == above, used, 0), axis=1, keepdims=True)

    def one(column, q):
        return lax.slice_in_dim(column, q, q + 1, axis=0)

    row = lax.broadcasted_iota(jnp.int32, (padded, 1), 0)
    wide_lane = lax.broadcasted_iota(jnp.int32, (padded, total), 1)
    wide_row = lax.broadcasted_iota(jnp.int32, (padded, total), 0)
    source = here - REACH + wide_row
    source = jnp.where(source < 0, source + total, source)
    source = jnp.where(source >= total, source - total, source)
    pick = (wide_lane == source).astype(jnp.float32)

    def picked(off):
        return lax.dot_general(
            pick, off.astype(jnp.float32), (((1,), (1,)), ((), ())),
            preferred_element_type=jnp.float32,
        ).astype(jnp.int32)

    dx, dp = picked(x_off), picked(p_off)
    x_row, p_row = masks(dx, BAND, 1), masks(dp, REACH, 1)
    far_row = jnp.zeros((padded, 1), jnp.int32)
    far_base = jnp.zeros((padded, 1), jnp.int32)
    sent = jnp.zeros((padded, 1), jnp.int32)
    base_low = jnp.zeros((1, 1), jnp.int32)
    base_high = jnp.full((1, 1), most, jnp.int32)
    for q in range(BAND):
        t = BAND - 1 - q
        low, high = one(at_here, t), one(at_above, BAND + q)
        place = padded - BAND + q
        far_row = jnp.where(row == t, low, jnp.where(row == place, high, far_row))
        far_base = jnp.where(row == t, base_low, jnp.where(row == place, base_high, far_base))
        base_low = base_low + bit_count(low)
        base_high = base_high + bit_count(high)
        sent = jnp.where(row == rows + t, one(at_above, t), sent)
        sent = jnp.where(row == REACH + BAND + q, one(at_here, BAND + q), sent)

    column = lax.broadcasted_iota(jnp.int32, (padded, LANES), 1)
    place = column & 31

    def looked_up(mask, reach):
        at = place - (CENTRE - reach)
        inside = (at >= 0) & (at <= 2 * reach)
        at = jnp.where(inside, at, 0)
        return inside & (((mask >> at) & 1) == 1), bit_count(mask & ((1 << at) - 1))

    close = (row >= BAND) & (row < padded - BAND)
    own = (row >= REACH) & (row < REACH + rows)
    x_hit, x_slot = looked_up(x_row, BAND)
    p_hit, p_slot = looked_up(p_row, REACH)
    far_hit, far_rank = looked_up(far_row, BAND)
    halo = jnp.where(row < REACH, row - BAND, row - rows - REACH + BAND) * pnz
    table = jnp.where(x_hit & close, row * nnz + x_slot, padded * nnz)
    to_gram = jnp.where(p_hit & own, (row - REACH) * pnz + p_slot, rows * pnz)
    to_far = jnp.where(far_hit, far_base + far_rank, 2 * most)
    to_halo = jnp.where(p_hit & close & ~own, halo + p_slot, edge)
    table = jnp.where(column >= TO_GRAM, to_gram, table)
    table = jnp.where(column >= TO_FAR, to_far, table)
    table = jnp.where(column >= TO_HALO, to_halo, table)
    for s in range(nnz):
        table = jnp.where(column == shift_lane(s), lax.slice_in_dim(dx, s, s + 1, axis=1), table)
    for p in range(pnz):
        table = jnp.where(column == want_lane(p), lax.slice_in_dim(dp, p, p + 1, axis=1), table)
    ints[...] = jnp.where(column == SENT, sent, table)


def products(dims, ints, r, slots, table, left, right, base=0):
    _, nnz, pnz = dims
    shift = {s: ints[r, shift_lane(s)] for s in slots}
    want = [ints[r, want_lane(p)] + CENTRE for p in range(pnz)]
    own = jnp.concatenate([left[r * nnz + s - base] for s in slots], axis=1)
    size = left.shape[1]
    blocks = []
    for p in range(0, pnz, 2):
        columns = [
            jnp.concatenate(
                [right[ints[r + shift[s], table + want[q] - shift[s]]] for s in slots], axis=0
            )
            for q in (p, p + 1)
        ]
        pair = jnp.dot(
            own, jnp.concatenate(columns, axis=1), preferred_element_type=jnp.float32
        )
        blocks += [pair[:, :size], pair[:, size:]]
    return blocks


def clear(ref):
    ref[ref.shape[0] - 1] = jnp.zeros(ref.shape[1:], ref.dtype)


def begin(sems, moves):
    copies = []
    for n, (source, target, place) in enumerate(moves):
        copy = pltpu.make_async_copy(
            source, target.at[pl.ds(place, source.shape[0])], sems.at[n]
        )
        copy.start()
        copies.append(copy)
    return copies


def finish(copies):
    for copy in copies:
        copy.wait()


def gather(dims, ints, side, skip, pool, out, picks, sem):
    rows, nnz, _ = dims
    top = REACH + rows - BAND - 1
    rows_sent = [top - q if side == 0 else REACH + BAND + q for q in range(BAND)]
    for n in range(skip + out.shape[0]):
        picks[n] = rows_sent[0] * nnz
    count = jnp.int32(0)
    for r in rows_sent:
        for s in range(nnz):
            picks[count] = r * nnz + s
            count = count + ((ints[r, SENT] >> (ints[r, shift_lane(s)] + BAND)) & 1)
    copies = []
    for n in range(out.shape[0]):
        copy = pltpu.make_async_copy(
            pool.at[pl.ds(picks[skip + n], 1)], out.at[pl.ds(n, 1)], sem.at[n]
        )
        copy.start()
        copies.append(copy)
    return copies


def in_pairs(count, step):
    @pl.loop(0, count // 2)
    def _(half):
        step(2 * half)
        step(2 * half + 1)


def gram_row(dims, scale, ints, i, pool, gram, place):
    pnz = dims[2]
    blocks = products(dims, ints, REACH + i, range(dims[1]), TO_X, pool, pool)
    for p, block in enumerate(blocks):
        gram[place * pnz + p] = (block * scale).astype(gram.dtype)


def update_row(dims, ints, i, pool, gram, target, place):
    pnz = dims[2]
    r = REACH + i
    blocks = products(dims, ints, r, range(dims[1]), TO_GRAM, pool, gram)
    for p, block in enumerate(blocks):
        kept = pool[ints[r, TO_X + ints[r, want_lane(p)] + CENTRE]].astype(jnp.float32)
        target[place * pnz + p] = (1.5 * kept - 0.5 * block).astype(target.dtype)


def crossing(dims, upper):
    rows, nnz, _ = dims
    if upper:
        spans = [(nnz - 1 - e, e + 1) for e in range(BAND)]
        listed = [rows + e for e in range(BAND)] + [rows - BAND + e for e in range(BAND)]
    else:
        spans = [(0, BAND - e) for e in range(BAND)]
        listed = [e - BAND for e in range(BAND)] + list(range(BAND))
    return [(row, *span) for row, span in zip(listed, spans + spans)]


def inner_kernel(
    dims, scale, ints, x, out, up, down, pool, gram, picks, sems, pick_sems
):
    rows, nnz, pnz = dims
    copies = begin(sems, [(x, pool, REACH * nnz)])
    clear(pool)
    finish(copies)
    listed = []
    for side, sent in enumerate((up, down)):
        listed += gather(dims, ints, side, 0, pool, sent, picks.at[side], pick_sems.at[side])
    in_pairs(rows - 2 * BAND, lambda n: gram_row(dims, scale, ints, BAND + n, pool, gram, n))
    finish(begin(sems, [(gram, out, 0)]) + listed)


def near_kernel(
    dims, scale, upper, ints, x, near, inner, *rest
):
    if upper:
        rest = rest[1:]
    out, part, gram_part, lefts, sent, *rest = rest
    pool, gram, done, kept_sums, near_sums, picks, sems, left_sems, pick_sems = rest
    rows, nnz, pnz = dims
    half, many = rows // 2, near.shape[0]
    start = REACH * nnz
    mine = half * nnz
    x_from = mine if upper else 0
    near_at = start + 2 * mine if upper else start - many
    copies = begin(sems, [
        (near, pool, near_at), (x.at[pl.ds(x_from, mine)], pool, start + x_from),
        (inner, gram, BAND * pnz),
    ])
    clear(pool)
    clear(gram)
    edge = rows - BAND if upper else 0
    halo = rows if upper else -BAND
    full = half if upper else BAND

    def halo_row(n):
        blocks = products(dims, ints, REACH + halo + n, range(nnz), TO_X, pool, pool)
        for p, block in enumerate(blocks):
            near_sums[n * pnz + p] = block

    finish(copies[:2])
    place, moves = 0, []
    for row, slot, count in crossing(dims, upper):
        moves.append((pool.at[pl.ds((REACH + row) * nnz + slot, count)], lefts, place))
        place += count
    laid = begin(left_sems, moves)
    side, skip = 0 if upper else 1, BAND * nnz - sent.shape[0]
    laid += gather(dims, ints, side, skip, pool, sent, picks, pick_sems)
    in_pairs(BAND, halo_row)
    first = begin(sems.at[pl.ds(0, 1)], [(near_sums, gram_part, 0)])
    finish(copies[2:])
    in_pairs(BAND, lambda n: gram_row(dims, scale, ints, edge + n, pool, gram, edge + n))
    in_pairs(BAND, lambda n: update_row(dims, ints, edge + n, pool, gram, kept_sums, n))
    second = begin(sems.at[pl.ds(1, 1)], [(kept_sums, part, 0)])
    in_pairs(half - BAND, lambda n: update_row(dims, ints, full + n, pool, gram, done, n))
    third = begin(sems.at[pl.ds(2, 1)], [(done, out, full * pnz)])
    finish(first + second + third + laid)


def far_kernel(
    dims, scale, ints, left_low, left_high, far_low, far_high, more, part_low, part_high,
    gram_low, gram_high, unused, out, left, far, gram, near_sums, kept_sums, done, sems
):
    rows, nnz, pnz = dims
    first = far_low.shape[0]
    extra = more.shape[0] // 2
    edge = BAND * pnz
    copies = begin(sems, [
        (left_low, left, 0),
        (left_high, left, left_low.shape[0]),
        (far_low, far, 0),
        (far_high, far, first + extra),
        (more.at[pl.ds(0, extra)], far, first),
        (more.at[pl.ds(extra, extra)], far, 2 * first + extra),
    ])
    late = begin(sems.at[pl.ds(len(copies), 4)], [
        (gram_low, near_sums, 0), (gram_high, near_sums, edge),
        (part_low, kept_sums, 0), (part_high, kept_sums, edge),
    ])
    used = len(copies) + len(late)
    clear(far)
    clear(gram)
    finish(copies)
    low_rows, high_rows = crossing(dims, False), crossing(dims, True)
    place, tasks = 0, []
    for row, slot, many in low_rows + high_rows:
        tasks.append((row, range(slot, slot + many), (REACH + row) * nnz + slot - place))
        place += many

    def group(listed, table, right, at, store):
        for e, (row, slots, base) in enumerate(listed):
            blocks = products(dims, ints, REACH + row, slots, table, left, right, base)
            for p, block in enumerate(blocks):
                store(at + e * pnz + p, block)

    def store_gram(n, block):
        gram[n] = ((near_sums[n] + block) * scale).astype(gram.dtype)

    def store_done(n, block):
        done[n] = (kept_sums[n] - 0.5 * block).astype(done.dtype)

    late[0].wait()
    group(tasks[:BAND], TO_FAR, far, 0, store_gram)
    late[1].wait()
    group(tasks[2 * BAND:3 * BAND], TO_FAR, far, edge, store_gram)
    late[2].wait()
    group(tasks[BAND:2 * BAND], TO_HALO, gram, 0, store_done)
    outgoing = begin(sems.at[pl.ds(used, 1)], [(done.at[pl.ds(0, edge)], out, 0)])
    late[3].wait()
    group(tasks[3 * BAND:], TO_HALO, gram, edge, store_done)
    outgoing += begin(
        sems.at[pl.ds(used + 1, 1)], [(done.at[pl.ds(edge, edge)], out, (rows - BAND) * pnz)]
    )
    finish(outgoing)


def body(x_vals, x_cols, p_cols):
    rows, nnz, size, _ = x_vals.shape
    pnz = p_cols.shape[1]
    count = lax.axis_size(AXES)
    me = lax.axis_index(AXES)
    first_row = me * rows
    scale = 1.0 / (4 * nnz * size)
    padded = rows + 2 * REACH
    forward = [(i, (i + 1) % count) for i in range(count)]
    backward = [(target, source) for source, target in forward]
    near = BAND * nnz
    edge = 2 * BAND * pnz
    most = near
    first = min(FIRST, most)
    product = 2 * size ** 3
    block = (size, size)

    smem = pl.BlockSpec(memory_space=pltpu.SMEM)
    hbm = pl.BlockSpec(memory_space=pl.ANY)
    vmem = pl.BlockSpec(memory_space=pltpu.VMEM)

    def shaped(blocks, kind=jnp.bfloat16):
        return jax.ShapeDtypeStruct((blocks,) + block, kind)

    def scratch(blocks, kind=jnp.bfloat16):
        return pltpu.VMEM((blocks,) + block, kind)

    def settings(mib):
        return pltpu.CompilerParams(vmem_limit_bytes=mib * MIB)

    def cost(products_made, blocks_moved):
        return pl.CostEstimate(
            flops=products_made * product, bytes_accessed=blocks_moved * 2 * size * size,
            transcendentals=0,
        )

    x = x_vals.reshape(rows * nnz, size, size)
    low = lax.ppermute(x[rows * nnz - near:], AXES, forward)
    high = lax.ppermute(x[:near], AXES, backward)

    dims = (rows, nnz, pnz)
    ints, largest = pl.pallas_call(
        partial(plan_kernel, dims),
        out_shape=(
            jax.ShapeDtypeStruct((padded, LANES), jnp.int32),
            jax.ShapeDtypeStruct((8, LANES), jnp.int32),
        ),
        in_specs=[smem, vmem, vmem],
        out_specs=(vmem, vmem),
        compiler_params=settings(BIG),
    )(me.astype(jnp.int32).reshape(1), x_cols.T, p_cols.T)
    largest = lax.pmax(largest[0, 0], "groups")

    lists = pltpu.SMEM((2, 32), jnp.int32)
    remaining = most - first
    inner, up, down = pl.pallas_call(
        partial(inner_kernel, dims, scale),
        out_shape=[
            shaped((rows - 2 * BAND) * pnz), shaped(first), shaped(first)
        ],
        in_specs=[smem, hbm],
        out_specs=[hbm] * 3,
        scratch_shapes=[
            scratch(padded * nnz + 1),
            scratch((rows - 2 * BAND) * pnz),
            lists,
            pltpu.SemaphoreType.DMA((1,)),
            pltpu.SemaphoreType.DMA((2, first)),
        ],
        compiler_params=settings(BIG),
        cost_estimate=cost((rows - 2 * BAND) * nnz * pnz, 200),
    )(ints, x)
    far_low = lax.ppermute(up, AXES, forward)
    far_high = lax.ppermute(down, AXES, backward)

    lefts_count = sum(span[2] for span in crossing(dims, False))

    def half_of_rows(upper, near_rows, *made):
        return pl.pallas_call(
            partial(near_kernel, dims, scale, upper),
            out_shape=[
                shaped(rows * pnz), shaped(edge // 2, jnp.float32),
                shaped(edge // 2, jnp.float32), shaped(lefts_count), shaped(remaining),
            ],
            in_specs=[smem] + [hbm] * (3 + len(made)),
            out_specs=[hbm] * 5,
            input_output_aliases={4: 0} if made else {},
            scratch_shapes=[
                scratch(padded * nnz + 1),
                scratch(rows * pnz + 1),
                scratch((rows // 2 - BAND) * pnz),
                scratch(edge // 2, jnp.float32),
                scratch(edge // 2, jnp.float32),
                pltpu.SMEM((32,), jnp.int32),
                pltpu.SemaphoreType.DMA((3,)),
                pltpu.SemaphoreType.DMA((2 * BAND,)),
                pltpu.SemaphoreType.DMA((remaining,)),
            ],
            compiler_params=settings(BIG),
            cost_estimate=cost((2 * BAND + rows // 2) * nnz * pnz, 500),
        )(ints, x, near_rows, inner, *made)

    out, part_low, gram_low, left_low, down_rest = half_of_rows(False, low)
    out, part_high, gram_high, left_high, up_rest = half_of_rows(True, high, out)

    def none_more(up, down):
        return jnp.zeros((2 * remaining,) + block, jnp.bfloat16)

    def all_more(up, down):
        return jnp.concatenate(
            [lax.ppermute(up, AXES, forward), lax.ppermute(down, AXES, backward)]
        )

    more = lax.cond(largest > first, all_more, none_more, up_rest, down_rest)

    operands = [
        ints, left_low, left_high, far_low, far_high, more, part_low, part_high, gram_low,
        gram_high, out,
    ]
    out = pl.pallas_call(
        partial(far_kernel, dims, scale),
        out_shape=shaped(rows * pnz),
        in_specs=[smem] + [hbm] * (len(operands) - 1),
        out_specs=hbm,
        input_output_aliases={len(operands) - 1: 0},
        scratch_shapes=[
            scratch(2 * lefts_count),
            scratch(2 * most + 1),
            scratch(edge + 1),
            scratch(edge, jnp.float32),
            scratch(edge, jnp.float32),
            scratch(edge),
            pltpu.SemaphoreType.DMA((12,)),
        ],
        compiler_params=settings(BIG),
        cost_estimate=cost(2 * BAND * nnz * pnz, 600),
    )(*operands)
    return out.reshape(rows, pnz, size, size)


def solution(mesh):
    return jax.shard_map(
        body,
        mesh=mesh,
        in_specs=(
            P(("groups", "grid", "rep"), None, None, None),
            P("groups", None),
            P("groups", None),
        ),
        out_specs=P(("groups", "grid", "rep"), None, None, None),
        check_vma=False,
    )
```

```python
from functools import partial

import jax
import jax.numpy as jnp
from jax import lax
from jax.experimental import pallas as pl
from jax.experimental.pallas import tpu as pltpu
from jax.sharding import PartitionSpec as P

BAND = 4
REACH = 2 * BAND
CENTRE = 3 * BAND
AXES = ("grid", "rep")
MIB = 1024 * 1024
FIRST = 16
BIG = 62
TO_X, TO_GRAM, TO_FAR, TO_HALO = 0, 32, 64, 96
LANES = 128
SPARE = 25
SENT = TO_HALO + SPARE


def shift_lane(s):
    return TO_X + SPARE + s


def want_lane(p):
    free = 32 - SPARE
    return (TO_GRAM + SPARE + p) if p < free else (TO_FAR + SPARE + p - free)


def bit_count(v):
    v = v - ((v >> 1) & 0x55555555)
    v = (v & 0x33333333) + ((v >> 2) & 0x33333333)
    v = (v + (v >> 4)) & 0x0F0F0F0F
    return (v + (v >> 8) + (v >> 16)) & 0x3F


def plan_kernel(dims, me, x_cols, p_cols, ints, largest):
    rows, nnz, pnz = dims
    total = x_cols.shape[1]
    padded = rows + 2 * REACH
    most = BAND * nnz
    edge = 2 * BAND * pnz
    lane = lax.broadcasted_iota(jnp.int32, (8, total), 1)
    sub = lax.broadcasted_iota(jnp.int32, (8, total), 0)

    def offsets(ref, count, reach):
        index = lax.broadcasted_iota(jnp.int32, (count, total), 1)
        off = ref[...] - index
        off = jnp.where(off < -reach, off + total, off)
        return jnp.where(off > reach, off - total, off)

    x_off, p_off = offsets(x_cols, nnz, BAND), offsets(p_cols, pnz, REACH)

    def masks(off, reach, axis):
        one = jnp.int32(1)
        parts = [
            lax.slice_in_dim(off, s, s + 1, axis=axis) for s in range(off.shape[axis])
        ]
        return sum(one << (part + reach) for part in parts)

    x_mask = jnp.broadcast_to(masks(x_off, BAND, 0), (8, total))
    p_mask = jnp.broadcast_to(masks(p_off, REACH, 0), (8, total))

    def framed(mask, t, left):
        return pltpu.roll(mask, (REACH - t) % total, 1) << left

    x_frame = [framed(x_mask, t, t) for t in range(2 * REACH)]
    p_frame = {t: framed(p_mask, t, t - BAND) for t in range(BAND, 3 * BAND)}

    def holds(mask, t):
        return -((mask >> (t + BAND)) & 1)

    def side(i, k, far):
        wanted = {}
        for tk in range(k, k + BAND):
            found = jnp.zeros_like(x_mask)
            for ti in range(i, i + BAND):
                found = found | (p_frame[ti] & holds(x_frame[ti], tk))
            wanted[tk] = found & p_frame[tk]
        used = []
        for tf in range(far, far + BAND):
            found = jnp.zeros_like(x_mask)
            for tk in range(k, k + BAND):
                found = found | (wanted[tk] & holds(x_frame[tk], tf))
            used.append((found & x_frame[tf]) >> tf)
        return used

    up, down = side(REACH, BAND, 0), side(BAND, REACH, 3 * BAND)
    needed = jnp.maximum(sum(map(bit_count, up)), sum(map(bit_count, down)))
    needed = jnp.where(lane % rows == 0, needed, 0)
    largest[...] = jnp.broadcast_to(jnp.max(needed, axis=(0, 1), keepdims=True), largest.shape)

    used = jnp.zeros_like(x_mask)
    for q, mask in enumerate(up + down):
        used = jnp.where(sub == q, mask, used)
    here = me[0] * rows
    above = jnp.where(here + rows == total, 0, here + rows)
    at_here = jnp.sum(jnp.where(lane == here, used, 0), axis=1, keepdims=True)
    at_above = jnp.sum(jnp.where(lane == above, used, 0), axis=1, keepdims=True)

    def one(column, q):
        return lax.slice_in_dim(column, q, q + 1, axis=0)

    row = lax.broadcasted_iota(jnp.int32, (padded, 1), 0)
    wide_lane = lax.broadcasted_iota(jnp.int32, (padded, total), 1)
    wide_row = lax.broadcasted_iota(jnp.int32, (padded, total), 0)
    source = here - REACH + wide_row
    source = jnp.where(source < 0, source + total, source)
    source = jnp.where(source >= total, source - total, source)
    pick = (wide_lane == source).astype(jnp.float32)

    def picked(off):
        return lax.dot_general(
            pick, off.astype(jnp.float32), (((1,), (1,)), ((), ())),
            preferred_element_type=jnp.float32,
        ).astype(jnp.int32)

    dx, dp = picked(x_off), picked(p_off)
    x_row, p_row = masks(dx, BAND, 1), masks(dp, REACH, 1)
    far_row = jnp.zeros((padded, 1), jnp.int32)
    far_base = jnp.zeros((padded, 1), jnp.int32)
    sent = jnp.zeros((padded, 1), jnp.int32)
    base_low = jnp.zeros((1, 1), jnp.int32)
    base_high = jnp.full((1, 1), most, jnp.int32)
    for q in range(BAND):
        t = BAND - 1 - q
        low, high = one(at_here, t), one(at_above, BAND + q)
        place = padded - BAND + q
        far_row = jnp.where(row == t, low, jnp.where(row == place, high, far_row))
        far_base = jnp.where(row == t, base_low, jnp.where(row == place, base_high, far_base))
        base_low = base_low + bit_count(low)
        base_high = base_high + bit_count(high)
        sent = jnp.where(row == rows + t, one(at_above, t), sent)
        sent = jnp.where(row == REACH + BAND + q, one(at_here, BAND + q), sent)

    column = lax.broadcasted_iota(jnp.int32, (padded, LANES), 1)
    place = column & 31

    def looked_up(mask, reach):
        at = place - (CENTRE - reach)
        inside = (at >= 0) & (at <= 2 * reach)
        at = jnp.where(inside, at, 0)
        return inside & (((mask >> at) & 1) == 1), bit_count(mask & ((1 << at) - 1))

    close = (row >= BAND) & (row < padded - BAND)
    own = (row >= REACH) & (row < REACH + rows)
    x_hit, x_slot = looked_up(x_row, BAND)
    p_hit, p_slot = looked_up(p_row, REACH)
    far_hit, far_rank = looked_up(far_row, BAND)
    halo = jnp.where(row < REACH, row - BAND, row - rows - REACH + BAND) * pnz
    table = jnp.where(x_hit & close, row * nnz + x_slot, padded * nnz)
    to_gram = jnp.where(p_hit & own, (row - REACH) * pnz + p_slot, rows * pnz)
    to_far = jnp.where(far_hit, far_base + far_rank, 2 * most)
    to_halo = jnp.where(p_hit & close & ~own, halo + p_slot, edge)
    table = jnp.where(column >= TO_GRAM, to_gram, table)
    table = jnp.where(column >= TO_FAR, to_far, table)
    table = jnp.where(column >= TO_HALO, to_halo, table)
    for s in range(nnz):
        table = jnp.where(column == shift_lane(s), lax.slice_in_dim(dx, s, s + 1, axis=1), table)
    for p in range(pnz):
        table = jnp.where(column == want_lane(p), lax.slice_in_dim(dp, p, p + 1, axis=1), table)
    ints[...] = jnp.where(column == SENT, sent, table)


def products(dims, ints, r, slots, table, left, right, base=0):
    _, nnz, pnz = dims
    shift = {s: ints[r, shift_lane(s)] for s in slots}
    want = [ints[r, want_lane(p)] + CENTRE for p in range(pnz)]
    own = jnp.concatenate([left[r * nnz + s - base] for s in slots], axis=1)
    size = left.shape[1]
    blocks = []
    for p in range(0, pnz, 2):
        columns = [
            jnp.concatenate(
                [right[ints[r + shift[s], table + want[q] - shift[s]]] for s in slots], axis=0
            )
            for q in (p, p + 1)
        ]
        pair = jnp.dot(
            own, jnp.concatenate(columns, axis=1), preferred_element_type=jnp.float32
        )
        blocks += [pair[:, :size], pair[:, size:]]
    return blocks


def clear(ref):
    ref[ref.shape[0] - 1] = jnp.zeros(ref.shape[1:], ref.dtype)


def begin(sems, moves):
    copies = []
    for n, (source, target, place) in enumerate(moves):
        copy = pltpu.make_async_copy(
            source, target.at[pl.ds(place, source.shape[0])], sems.at[n]
        )
        copy.start()
        copies.append(copy)
    return copies


def table_copy(source, ints, sem):
    copy = pltpu.make_async_copy(source, ints, sem.at[0])
    copy.start()
    return copy


def finish(copies):
    for copy in copies:
        copy.wait()


def gather(dims, ints, side, skip, pool, out, picks, sem):
    rows, nnz, _ = dims
    top = REACH + rows - BAND - 1
    rows_sent = [top - q if side == 0 else REACH + BAND + q for q in range(BAND)]
    for n in range(skip + out.shape[0]):
        picks[n] = rows_sent[0] * nnz
    count = jnp.int32(0)
    for r in rows_sent:
        for s in range(nnz):
            picks[count] = r * nnz + s
            count = count + ((ints[r, SENT] >> (ints[r, shift_lane(s)] + BAND)) & 1)
    copies = []
    for n in range(out.shape[0]):
        copy = pltpu.make_async_copy(
            pool.at[pl.ds(picks[skip + n], 1)], out.at[pl.ds(n, 1)], sem.at[n]
        )
        copy.start()
        copies.append(copy)
    return copies


def in_pairs(count, step):
    @pl.loop(0, count // 2)
    def _(half):
        step(2 * half)
        step(2 * half + 1)


def gram_row(dims, scale, ints, i, pool, gram, place):
    pnz = dims[2]
    blocks = products(dims, ints, REACH + i, range(dims[1]), TO_X, pool, pool)
    for p, block in enumerate(blocks):
        gram[place * pnz + p] = (block * scale).astype(gram.dtype)


def update_row(dims, ints, i, pool, gram, target, place):
    pnz = dims[2]
    r = REACH + i
    blocks = products(dims, ints, r, range(dims[1]), TO_GRAM, pool, gram)
    for p, block in enumerate(blocks):
        kept = pool[ints[r, TO_X + ints[r, want_lane(p)] + CENTRE]].astype(jnp.float32)
        target[place * pnz + p] = (1.5 * kept - 0.5 * block).astype(target.dtype)


def crossing(dims, upper):
    rows, nnz, _ = dims
    if upper:
        spans = [(nnz - 1 - e, e + 1) for e in range(BAND)]
        listed = [rows + e for e in range(BAND)] + [rows - BAND + e for e in range(BAND)]
    else:
        spans = [(0, BAND - e) for e in range(BAND)]
        listed = [e - BAND for e in range(BAND)] + list(range(BAND))
    return [(row, *span) for row, span in zip(listed, spans + spans)]


def inner_kernel(
    dims, scale, table, x, out, up, down, ints, pool, gram, picks, table_sem, sems, pick_sems
):
    rows, nnz, pnz = dims
    copies = [table_copy(table, ints, table_sem)] + begin(sems, [(x, pool, REACH * nnz)])
    clear(pool)
    finish(copies)
    listed = []
    for side, sent in enumerate((up, down)):
        listed += gather(dims, ints, side, 0, pool, sent, picks.at[side], pick_sems.at[side])
    in_pairs(rows - 2 * BAND, lambda n: gram_row(dims, scale, ints, BAND + n, pool, gram, n))
    finish(begin(sems, [(gram, out, 0)]) + listed)


def near_kernel(dims, scale, upper, table, x, near, inner, *rest):
    out, part, gram_part, sent, lefts, ints, *scratch = rest[-16:]
    pool, gram, done, own_sums, near_sums, picks, table_sem, sems, pick_sems, left_sems = scratch
    rows, nnz, pnz = dims
    half, many = rows // 2, near.shape[0]
    start = REACH * nnz
    mine = half * nnz
    x_from = mine if upper else 0
    near_at = start + 2 * mine if upper else start - many
    copies = [table_copy(table, ints, table_sem)] + begin(sems, [
        (near, pool, near_at), (x.at[pl.ds(x_from, mine)], pool, start + x_from),
        (inner, gram, BAND * pnz),
    ])
    clear(pool)
    clear(gram)
    edge = rows - BAND if upper else 0
    halo = rows if upper else -BAND
    full = half if upper else BAND

    def halo_row(n):
        blocks = products(dims, ints, REACH + halo + n, range(nnz), TO_X, pool, pool)
        for p, block in enumerate(blocks):
            near_sums[n * pnz + p] = block.astype(near_sums.dtype)

    def edge_row(n):
        blocks = products(dims, ints, REACH + edge + n, range(nnz), TO_GRAM, pool, gram)
        for p, block in enumerate(blocks):
            own_sums[n * pnz + p] = block.astype(own_sums.dtype)

    finish(copies[:3])
    side, skip = 0 if upper else 1, BAND * nnz - sent.shape[0]
    laid = gather(dims, ints, side, skip, pool, sent, picks, pick_sems)
    place, moves = 0, []
    for row, slot, count in crossing(dims, upper)[:BAND]:
        moves.append((pool.at[pl.ds((REACH + row) * nnz + slot, count)], lefts, place))
        place += count
    laid += begin(left_sems, moves)
    in_pairs(BAND, halo_row)
    first = begin(sems.at[pl.ds(0, 1)], [(near_sums, gram_part, 0)])
    finish(copies[3:])
    in_pairs(BAND, lambda n: gram_row(dims, scale, ints, edge + n, pool, gram, edge + n))
    in_pairs(BAND, edge_row)
    second = begin(sems.at[pl.ds(1, 1)], [(own_sums, part, 0)])
    in_pairs(half - BAND, lambda n: update_row(dims, ints, full + n, pool, gram, done, n))
    third = begin(sems.at[pl.ds(2, 1)], [(done, out, full * pnz)])
    finish(first + second + third + laid)


def far_kernel(
    dims, scale, table, x, left_low, left_high, far_low, far_high, more_low, more_high, gram_low, gram_high,
    part_low, part_high, unused, out, ints, pool, far, gram, near_sums, own_sums, done, table_sem,
    sems
):
    rows, nnz, pnz = dims
    first, near, own = far_low.shape[0], BAND * nnz, x.shape[0]
    edge = BAND * pnz
    start = REACH * nnz
    moves = [
        (far_low, far, 0), (more_low, far, first),
        (far_high, far, near), (more_high, far, near + first),
    ]
    for upper, lefts in ((False, left_low), (True, left_high)):
        place = 0
        for row, slot, many in crossing(dims, upper)[:BAND]:
            moves.append((lefts.at[pl.ds(place, many)], pool, (REACH + row) * nnz + slot))
            place += many
    early = [table_copy(table, ints, table_sem)] + begin(sems, moves)
    late = begin(sems.at[pl.ds(len(moves), 6)], [
        (gram_low, near_sums, 0), (gram_high, near_sums, edge),
        (x.at[pl.ds(0, near)], pool, start), (part_low, own_sums, 0),
        (x.at[pl.ds(own - near, near)], pool, start + own - near), (part_high, own_sums, edge),
    ])
    used = len(moves) + len(late)
    clear(pool)
    clear(far)
    clear(gram)
    finish(early)

    def far_terms(upper):
        for e, (row, slot, many) in enumerate(crossing(dims, upper)[:BAND]):
            slots = range(slot, slot + many)
            blocks = products(dims, ints, REACH + row, slots, TO_FAR, pool, far)
            for p, block in enumerate(blocks):
                n = (upper * BAND + e) * pnz + p
                whole = near_sums[n].astype(jnp.float32) + block
                gram[n] = (whole * scale).astype(gram.dtype)

    def halo_terms(upper, places):
        for e in places:
            row, slot, many = crossing(dims, upper)[BAND + e]
            r = REACH + row
            slots = range(slot, slot + many)
            blocks = products(dims, ints, r, slots, TO_HALO, pool, gram)
            for p, block in enumerate(blocks):
                n = (upper * BAND + e) * pnz + p
                kept = pool[ints[r, TO_X + ints[r, want_lane(p)] + CENTRE]].astype(jnp.float32)
                whole = own_sums[n].astype(jnp.float32) + block
                done[n] = (1.5 * kept - 0.5 * whole).astype(done.dtype)
        at, many = (upper * BAND + places[0]) * pnz, len(places) * pnz
        place = (places[0] + (rows - BAND if upper else 0)) * pnz
        return begin(
            sems.at[pl.ds(used + 2 * upper + places[0] // 2, 1)],
            [(done.at[pl.ds(at, many)], out, place)],
        )

    finish(late[:1])
    far_terms(False)
    finish(late[1:2])
    far_terms(True)
    finish(late[2:4])
    half = BAND // 2
    outgoing = halo_terms(False, range(BAND))
    finish(late[4:])
    outgoing += halo_terms(True, range(half, BAND))
    outgoing += halo_terms(True, range(half))
    finish(outgoing)


def body(x_vals, x_cols, p_cols):
    rows, nnz, size, _ = x_vals.shape
    pnz = p_cols.shape[1]
    count = lax.axis_size(AXES)
    me = lax.axis_index(AXES)
    first_row = me * rows
    scale = 1.0 / (4 * nnz * size)
    padded = rows + 2 * REACH
    forward = [(i, (i + 1) % count) for i in range(count)]
    backward = [(target, source) for source, target in forward]
    near = BAND * nnz
    edge = 2 * BAND * pnz
    most = near
    first = min(FIRST, most)
    product = 2 * size ** 3
    block = (size, size)

    smem = pl.BlockSpec(memory_space=pltpu.SMEM)
    hbm = pl.BlockSpec(memory_space=pl.ANY)
    vmem = pl.BlockSpec(memory_space=pltpu.VMEM)

    def shaped(blocks, kind=jnp.bfloat16):
        return jax.ShapeDtypeStruct((blocks,) + block, kind)

    def scratch(blocks, kind=jnp.bfloat16):
        return pltpu.VMEM((blocks,) + block, kind)

    def settings(mib):
        return pltpu.CompilerParams(vmem_limit_bytes=mib * MIB)

    def cost(products_made, blocks_moved):
        return pl.CostEstimate(
            flops=products_made * product, bytes_accessed=blocks_moved * 2 * size * size,
            transcendentals=0,
        )

    x = x_vals.reshape(rows * nnz, size, size)
    low = lax.ppermute(x[rows * nnz - near:], AXES, forward)
    high = lax.ppermute(x[:near], AXES, backward)

    dims = (rows, nnz, pnz)
    ints, largest = pl.pallas_call(
        partial(plan_kernel, dims),
        out_shape=(
            jax.ShapeDtypeStruct((padded, LANES), jnp.int32),
            jax.ShapeDtypeStruct((8, LANES), jnp.int32),
        ),
        in_specs=[smem, vmem, vmem],
        out_specs=(vmem, vmem),
        compiler_params=settings(BIG),
    )(me.astype(jnp.int32).reshape(1), x_cols.T, p_cols.T)
    largest = lax.pmax(largest[0, 0], "groups")

    lists = pltpu.SMEM((2, 32), jnp.int32)
    table = pltpu.SMEM((padded, LANES), jnp.int32)
    remaining = most - first
    inner, up, down = pl.pallas_call(
        partial(inner_kernel, dims, scale),
        out_shape=[
            shaped((rows - 2 * BAND) * pnz), shaped(first), shaped(first)
        ],
        in_specs=[hbm, hbm],
        out_specs=[hbm] * 3,
        scratch_shapes=[
            table,
            scratch(padded * nnz + 1),
            scratch((rows - 2 * BAND) * pnz),
            lists,
            pltpu.SemaphoreType.DMA((1,)),
            pltpu.SemaphoreType.DMA((1,)),
            pltpu.SemaphoreType.DMA((2, first)),
        ],
        compiler_params=settings(BIG),
        cost_estimate=cost((rows - 2 * BAND) * nnz * pnz, 200),
    )(ints, x)
    far_low = lax.ppermute(up, AXES, forward)
    far_high = lax.ppermute(down, AXES, backward)

    half_edge = BAND * pnz
    lefts_count = sum(span[2] for span in crossing(dims, False)[:BAND])

    def half_of_rows(upper, near_rows, *made):
        return pl.pallas_call(
            partial(near_kernel, dims, scale, upper),
            out_shape=[
                shaped(rows * pnz), shaped(half_edge), shaped(half_edge), shaped(remaining),
                shaped(lefts_count),
            ],
            in_specs=[hbm] * (4 + len(made)),
            out_specs=[hbm] * 5,
            input_output_aliases={4: 0} if made else {},
            scratch_shapes=[
                table,
                scratch(padded * nnz + 1),
                scratch(rows * pnz + 1),
                scratch((rows // 2 - BAND) * pnz),
                scratch(half_edge),
                scratch(half_edge),
                pltpu.SMEM((32,), jnp.int32),
                pltpu.SemaphoreType.DMA((1,)),
                pltpu.SemaphoreType.DMA((3,)),
                pltpu.SemaphoreType.DMA((remaining,)),
                pltpu.SemaphoreType.DMA((BAND,)),
            ],
            compiler_params=settings(BIG),
            cost_estimate=cost((2 * BAND + rows // 2) * nnz * pnz, 500),
        )(ints, x, near_rows, inner, *made)

    out, part_low, gram_low, down_rest, left_low = half_of_rows(False, low)
    out, part_high, gram_high, up_rest, left_high = half_of_rows(True, high, out)

    def send_rest(state):
        _, up, down = state
        return False, lax.ppermute(up, AXES, forward), lax.ppermute(down, AXES, backward)

    _, more_low, more_high = lax.while_loop(
        lambda state: state[0], send_rest, (largest > first, up_rest, down_rest)
    )

    operands = [
        ints, x, left_low, left_high, far_low, far_high, more_low, more_high, gram_low, gram_high, part_low,
        part_high, out,
    ]
    out = pl.pallas_call(
        partial(far_kernel, dims, scale),
        out_shape=shaped(rows * pnz),
        in_specs=[hbm] * len(operands),
        out_specs=hbm,
        input_output_aliases={len(operands) - 1: 0},
        scratch_shapes=[
            table,
            scratch(padded * nnz + 1),
            scratch(2 * most + 1),
            scratch(edge + 1),
            scratch(edge),
            scratch(edge),
            scratch(edge),
            pltpu.SemaphoreType.DMA((1,)),
            pltpu.SemaphoreType.DMA((14 + 2 * BAND,)),
        ],
        compiler_params=settings(BIG),
        cost_estimate=cost(2 * BAND * nnz * pnz, 400),
    )(*operands)
    return out.reshape(rows, pnz, size, size)


def solution(mesh):
    return jax.shard_map(
        body,
        mesh=mesh,
        in_specs=(
            P(("groups", "grid", "rep"), None, None, None),
            P("groups", None),
            P("groups", None),
        ),
        out_specs=P(("groups", "grid", "rep"), None, None, None),
        check_vma=False,
    )
```

```python
from functools import partial

import jax
import jax.numpy as jnp
from jax import lax
from jax.experimental import pallas as pl
from jax.experimental.pallas import tpu as pltpu
from jax.sharding import PartitionSpec as P

BAND = 4
REACH = 2 * BAND
CENTRE = 3 * BAND
AXES = ("grid", "rep")
MIB = 1024 * 1024
FIRST = 16
BIG = 62
TO_X, TO_GRAM, TO_FAR, TO_HALO = 0, 32, 64, 96
LANES = 128
SPARE = 25
SENT = TO_HALO + SPARE


def shift_lane(s):
    return TO_X + SPARE + s


def want_lane(p):
    free = 32 - SPARE
    return (TO_GRAM + SPARE + p) if p < free else (TO_FAR + SPARE + p - free)


def bit_count(v):
    v = v - ((v >> 1) & 0x55555555)
    v = (v & 0x33333333) + ((v >> 2) & 0x33333333)
    v = (v + (v >> 4)) & 0x0F0F0F0F
    return (v + (v >> 8) + (v >> 16)) & 0x3F


def plan_kernel(dims, me, x_cols, p_cols, ints, largest):
    rows, nnz, pnz = dims
    total = x_cols.shape[1]
    padded = rows + 2 * REACH
    most = BAND * nnz
    edge = 2 * BAND * pnz
    lane = lax.broadcasted_iota(jnp.int32, (8, total), 1)
    sub = lax.broadcasted_iota(jnp.int32, (8, total), 0)

    def offsets(ref, count, reach):
        index = lax.broadcasted_iota(jnp.int32, (count, total), 1)
        off = ref[...] - index
        off = jnp.where(off < -reach, off + total, off)
        return jnp.where(off > reach, off - total, off)

    x_off, p_off = offsets(x_cols, nnz, BAND), offsets(p_cols, pnz, REACH)

    def masks(off, reach, axis):
        one = jnp.int32(1)
        parts = [
            lax.slice_in_dim(off, s, s + 1, axis=axis) for s in range(off.shape[axis])
        ]
        return sum(one << (part + reach) for part in parts)

    x_mask = jnp.broadcast_to(masks(x_off, BAND, 0), (8, total))
    p_mask = jnp.broadcast_to(masks(p_off, REACH, 0), (8, total))

    def framed(mask, t, left):
        return pltpu.roll(mask, (REACH - t) % total, 1) << left

    x_frame = [framed(x_mask, t, t) for t in range(2 * REACH)]
    p_frame = {t: framed(p_mask, t, t - BAND) for t in range(BAND, 3 * BAND)}

    def holds(mask, t):
        return -((mask >> (t + BAND)) & 1)

    def side(i, k, far):
        wanted = {}
        for tk in range(k, k + BAND):
            found = jnp.zeros_like(x_mask)
            for ti in range(i, i + BAND):
                found = found | (p_frame[ti] & holds(x_frame[ti], tk))
            wanted[tk] = found & p_frame[tk]
        used = []
        for tf in range(far, far + BAND):
            found = jnp.zeros_like(x_mask)
            for tk in range(k, k + BAND):
                found = found | (wanted[tk] & holds(x_frame[tk], tf))
            used.append((found & x_frame[tf]) >> tf)
        return used

    up, down = side(REACH, BAND, 0), side(BAND, REACH, 3 * BAND)
    needed = jnp.maximum(sum(map(bit_count, up)), sum(map(bit_count, down)))
    needed = jnp.where(lane % rows == 0, needed, 0)
    largest[...] = jnp.broadcast_to(jnp.max(needed, axis=(0, 1), keepdims=True), largest.shape)

    used = jnp.zeros_like(x_mask)
    for q, mask in enumerate(up + down):
        used = jnp.where(sub == q, mask, used)
    here = me[0] * rows
    above = jnp.where(here + rows == total, 0, here + rows)
    at_here = jnp.sum(jnp.where(lane == here, used, 0), axis=1, keepdims=True)
    at_above = jnp.sum(jnp.where(lane == above, used, 0), axis=1, keepdims=True)

    def one(column, q):
        return lax.slice_in_dim(column, q, q + 1, axis=0)

    row = lax.broadcasted_iota(jnp.int32, (padded, 1), 0)
    wide_lane = lax.broadcasted_iota(jnp.int32, (padded, total), 1)
    wide_row = lax.broadcasted_iota(jnp.int32, (padded, total), 0)
    source = here - REACH + wide_row
    source = jnp.where(source < 0, source + total, source)
    source = jnp.where(source >= total, source - total, source)
    pick = (wide_lane == source).astype(jnp.float32)

    def picked(off):
        return lax.dot_general(
            pick, off.astype(jnp.float32), (((1,), (1,)), ((), ())),
            preferred_element_type=jnp.float32,
        ).astype(jnp.int32)

    dx, dp = picked(x_off), picked(p_off)
    x_row, p_row = masks(dx, BAND, 1), masks(dp, REACH, 1)
    far_row = jnp.zeros((padded, 1), jnp.int32)
    far_base = jnp.zeros((padded, 1), jnp.int32)
    sent = jnp.zeros((padded, 1), jnp.int32)
    base_low = jnp.zeros((1, 1), jnp.int32)
    base_high = jnp.full((1, 1), most, jnp.int32)
    for q in range(BAND):
        t = BAND - 1 - q
        low, high = one(at_here, t), one(at_above, BAND + q)
        place = padded - BAND + q
        far_row = jnp.where(row == t, low, jnp.where(row == place, high, far_row))
        far_base = jnp.where(row == t, base_low, jnp.where(row == place, base_high, far_base))
        base_low = base_low + bit_count(low)
        base_high = base_high + bit_count(high)
        sent = jnp.where(row == rows + t, one(at_above, t), sent)
        sent = jnp.where(row == REACH + BAND + q, one(at_here, BAND + q), sent)

    column = lax.broadcasted_iota(jnp.int32, (padded, LANES), 1)
    place = column & 31

    def looked_up(mask, reach):
        at = place - (CENTRE - reach)
        inside = (at >= 0) & (at <= 2 * reach)
        at = jnp.where(inside, at, 0)
        return inside & (((mask >> at) & 1) == 1), bit_count(mask & ((1 << at) - 1))

    close = (row >= BAND) & (row < padded - BAND)
    own = (row >= REACH) & (row < REACH + rows)
    x_hit, x_slot = looked_up(x_row, BAND)
    p_hit, p_slot = looked_up(p_row, REACH)
    far_hit, far_rank = looked_up(far_row, BAND)
    halo = jnp.where(row < REACH, row - BAND, row - rows - REACH + BAND) * pnz
    table = jnp.where(x_hit & close, row * nnz + x_slot, padded * nnz)
    to_gram = jnp.where(p_hit & own, (row - REACH) * pnz + p_slot, rows * pnz)
    to_far = jnp.where(far_hit, far_base + far_rank, 2 * most)
    to_halo = jnp.where(p_hit & close & ~own, halo + p_slot, edge)
    table = jnp.where(column >= TO_GRAM, to_gram, table)
    table = jnp.where(column >= TO_FAR, to_far, table)
    table = jnp.where(column >= TO_HALO, to_halo, table)
    for s in range(nnz):
        table = jnp.where(column == shift_lane(s), lax.slice_in_dim(dx, s, s + 1, axis=1), table)
    for p in range(pnz):
        table = jnp.where(column == want_lane(p), lax.slice_in_dim(dp, p, p + 1, axis=1), table)
    ints[...] = jnp.where(column == SENT, sent, table)


def products(dims, ints, r, slots, table, left, right, base=0):
    _, nnz, pnz = dims
    shift = {s: ints[r, shift_lane(s)] for s in slots}
    want = [ints[r, want_lane(p)] + CENTRE for p in range(pnz)]
    own = jnp.concatenate([left[r * nnz + s - base] for s in slots], axis=1)
    size = left.shape[1]
    blocks = []
    for p in range(0, pnz, 2):
        columns = [
            jnp.concatenate(
                [right[ints[r + shift[s], table + want[q] - shift[s]]] for s in slots], axis=0
            )
            for q in (p, p + 1)
        ]
        pair = jnp.dot(
            own, jnp.concatenate(columns, axis=1), preferred_element_type=jnp.float32
        )
        blocks += [pair[:, :size], pair[:, size:]]
    return blocks


def clear(ref):
    ref[ref.shape[0] - 1] = jnp.zeros(ref.shape[1:], ref.dtype)


def begin(sems, moves):
    copies = []
    for n, (source, target, place) in enumerate(moves):
        copy = pltpu.make_async_copy(
            source, target.at[pl.ds(place, source.shape[0])], sems.at[n]
        )
        copy.start()
        copies.append(copy)
    return copies


def table_copy(source, ints, sem):
    copy = pltpu.make_async_copy(source, ints, sem.at[0])
    copy.start()
    return copy


def finish(copies):
    for copy in copies:
        copy.wait()


def gather(dims, ints, side, skip, pool, out, picks, sem):
    rows, nnz, _ = dims
    top = REACH + rows - BAND - 1
    rows_sent = [top - q if side == 0 else REACH + BAND + q for q in range(BAND)]
    for n in range(skip + out.shape[0]):
        picks[n] = rows_sent[0] * nnz
    count = jnp.int32(0)
    for r in rows_sent:
        for s in range(nnz):
            picks[count] = r * nnz + s
            count = count + ((ints[r, SENT] >> (ints[r, shift_lane(s)] + BAND)) & 1)
    copies = []
    for n in range(out.shape[0]):
        copy = pltpu.make_async_copy(
            pool.at[pl.ds(picks[skip + n], 1)], out.at[pl.ds(n, 1)], sem.at[n]
        )
        copy.start()
        copies.append(copy)
    return copies


def in_pairs(count, step):
    @pl.loop(0, count // 2)
    def _(half):
        step(2 * half)
        step(2 * half + 1)


def gram_row(dims, scale, ints, i, pool, gram, place):
    pnz = dims[2]
    blocks = products(dims, ints, REACH + i, range(dims[1]), TO_X, pool, pool)
    for p, block in enumerate(blocks):
        gram[place * pnz + p] = (block * scale).astype(gram.dtype)


def update_row(dims, ints, i, pool, gram, target, place):
    pnz = dims[2]
    r = REACH + i
    blocks = products(dims, ints, r, range(dims[1]), TO_GRAM, pool, gram)
    for p, block in enumerate(blocks):
        kept = pool[ints[r, TO_X + ints[r, want_lane(p)] + CENTRE]].astype(jnp.float32)
        target[place * pnz + p] = (1.5 * kept - 0.5 * block).astype(target.dtype)


def crossing(dims, upper):
    rows, nnz, _ = dims
    if upper:
        spans = [(nnz - 1 - e, e + 1) for e in range(BAND)]
        listed = [rows + e for e in range(BAND)] + [rows - BAND + e for e in range(BAND)]
    else:
        spans = [(0, BAND - e) for e in range(BAND)]
        listed = [e - BAND for e in range(BAND)] + list(range(BAND))
    return [(row, *span) for row, span in zip(listed, spans + spans)]


def inner_kernel(
    dims, scale, table, x, out, up, down, ints, pool, gram, picks, table_sem, sems, pick_sems
):
    rows, nnz, pnz = dims
    copies = [table_copy(table, ints, table_sem)] + begin(sems, [(x, pool, REACH * nnz)])
    clear(pool)
    finish(copies)
    listed = []
    for side, sent in enumerate((up, down)):
        listed += gather(dims, ints, side, 0, pool, sent, picks.at[side], pick_sems.at[side])
    in_pairs(rows - 2 * BAND, lambda n: gram_row(dims, scale, ints, BAND + n, pool, gram, n))
    finish(begin(sems, [(gram, out, 0)]) + listed)


def near_kernel(dims, scale, upper, table, x, near, inner, *rest):
    out, part, gram_part, sent, lefts, ints, *scratch = rest[-16:]
    pool, gram, done, own_sums, near_sums, picks, table_sem, sems, pick_sems, left_sems = scratch
    rows, nnz, pnz = dims
    half, many = rows // 2, near.shape[0]
    start = REACH * nnz
    mine = half * nnz
    x_from = mine if upper else 0
    near_at = start + 2 * mine if upper else start - many
    copies = [table_copy(table, ints, table_sem)] + begin(sems, [
        (near, pool, near_at), (x.at[pl.ds(x_from, mine)], pool, start + x_from),
        (inner, gram, BAND * pnz),
    ])
    clear(pool)
    clear(gram)
    edge = rows - BAND if upper else 0
    halo = rows if upper else -BAND
    full = half if upper else BAND

    def halo_row(n):
        blocks = products(dims, ints, REACH + halo + n, range(nnz), TO_X, pool, pool)
        for p, block in enumerate(blocks):
            near_sums[n * pnz + p] = block.astype(near_sums.dtype)

    def edge_row(n):
        blocks = products(dims, ints, REACH + edge + n, range(nnz), TO_GRAM, pool, gram)
        for p, block in enumerate(blocks):
            own_sums[n * pnz + p] = block.astype(own_sums.dtype)

    finish(copies[:3])
    side, skip = 0 if upper else 1, BAND * nnz - sent.shape[0]
    laid = gather(dims, ints, side, skip, pool, sent, picks, pick_sems)
    place, moves = 0, []
    for row, slot, count in crossing(dims, upper)[:BAND]:
        moves.append((pool.at[pl.ds((REACH + row) * nnz + slot, count)], lefts, place))
        place += count
    laid += begin(left_sems, moves)
    in_pairs(BAND, halo_row)
    first = begin(sems.at[pl.ds(0, 1)], [(near_sums, gram_part, 0)])
    finish(copies[3:])
    in_pairs(BAND, lambda n: gram_row(dims, scale, ints, edge + n, pool, gram, edge + n))
    in_pairs(BAND, edge_row)
    second = begin(sems.at[pl.ds(1, 1)], [(own_sums, part, 0)])
    in_pairs(half - BAND, lambda n: update_row(dims, ints, full + n, pool, gram, done, n))
    third = begin(sems.at[pl.ds(2, 1)], [(done, out, full * pnz)])
    finish(first + second + third + laid)


def far_kernel(
    dims, scale, table, x, left_low, left_high, far_low, far_high, more_low, more_high, gram_low, gram_high,
    part_low, part_high, unused, out, ints, pool, far, gram, near_sums, own_sums, done, table_sem,
    sems
):
    rows, nnz, pnz = dims
    first, near, own = far_low.shape[0], BAND * nnz, x.shape[0]
    edge = BAND * pnz
    start = REACH * nnz
    moves = [
        (far_low, far, 0), (more_low, far, first),
        (far_high, far, near), (more_high, far, near + first),
    ]
    for upper, lefts in ((False, left_low), (True, left_high)):
        place = 0
        for row, slot, many in crossing(dims, upper)[:BAND]:
            moves.append((lefts.at[pl.ds(place, many)], pool, (REACH + row) * nnz + slot))
            place += many
    early = [table_copy(table, ints, table_sem)] + begin(sems, moves)
    late = begin(sems.at[pl.ds(len(moves), 6)], [
        (gram_low, near_sums, 0), (gram_high, near_sums, edge),
        (x.at[pl.ds(0, near)], pool, start), (part_low, own_sums, 0),
        (x.at[pl.ds(own - near, near)], pool, start + own - near), (part_high, own_sums, edge),
    ])
    used = len(moves) + len(late)
    clear(pool)
    clear(far)
    clear(gram)
    finish(early)

    def far_terms(upper):
        for e, (row, slot, many) in enumerate(crossing(dims, upper)[:BAND]):
            slots = range(slot, slot + many)
            blocks = products(dims, ints, REACH + row, slots, TO_FAR, pool, far)
            for p, block in enumerate(blocks):
                n = (upper * BAND + e) * pnz + p
                whole = near_sums[n].astype(jnp.float32) + block
                gram[n] = (whole * scale).astype(gram.dtype)

    def halo_terms(upper, places):
        for e in places:
            row, slot, many = crossing(dims, upper)[BAND + e]
            r = REACH + row
            slots = range(slot, slot + many)
            blocks = products(dims, ints, r, slots, TO_HALO, pool, gram)
            for p, block in enumerate(blocks):
                n = (upper * BAND + e) * pnz + p
                kept = pool[ints[r, TO_X + ints[r, want_lane(p)] + CENTRE]].astype(jnp.float32)
                whole = own_sums[n].astype(jnp.float32) + block
                done[n] = (1.5 * kept - 0.5 * whole).astype(done.dtype)
        at, many = (upper * BAND + places[0]) * pnz, len(places) * pnz
        place = (places[0] + (rows - BAND if upper else 0)) * pnz
        return begin(
            sems.at[pl.ds(used + 2 * upper + places[0] // 2, 1)],
            [(done.at[pl.ds(at, many)], out, place)],
        )

    finish(late[:1])
    far_terms(False)
    finish(late[1:2])
    far_terms(True)
    finish(late[2:4])
    half = BAND // 2
    outgoing = halo_terms(False, range(BAND))
    finish(late[4:])
    outgoing += halo_terms(True, range(BAND))
    finish(outgoing)


def body(x_vals, x_cols, p_cols):
    rows, nnz, size, _ = x_vals.shape
    pnz = p_cols.shape[1]
    count = lax.axis_size(AXES)
    me = lax.axis_index(AXES)
    first_row = me * rows
    scale = 1.0 / (4 * nnz * size)
    padded = rows + 2 * REACH
    forward = [(i, (i + 1) % count) for i in range(count)]
    backward = [(target, source) for source, target in forward]
    near = BAND * nnz
    edge = 2 * BAND * pnz
    most = near
    first = min(FIRST, most)
    product = 2 * size ** 3
    block = (size, size)

    smem = pl.BlockSpec(memory_space=pltpu.SMEM)
    hbm = pl.BlockSpec(memory_space=pl.ANY)
    vmem = pl.BlockSpec(memory_space=pltpu.VMEM)

    def shaped(blocks, kind=jnp.bfloat16):
        return jax.ShapeDtypeStruct((blocks,) + block, kind)

    def scratch(blocks, kind=jnp.bfloat16):
        return pltpu.VMEM((blocks,) + block, kind)

    def settings(mib):
        return pltpu.CompilerParams(vmem_limit_bytes=mib * MIB)

    def cost(products_made, blocks_moved):
        return pl.CostEstimate(
            flops=products_made * product, bytes_accessed=blocks_moved * 2 * size * size,
            transcendentals=0,
        )

    x = x_vals.reshape(rows * nnz, size, size)
    low = lax.ppermute(x[rows * nnz - near:], AXES, forward)
    high = lax.ppermute(x[:near], AXES, backward)

    dims = (rows, nnz, pnz)
    ints, largest = pl.pallas_call(
        partial(plan_kernel, dims),
        out_shape=(
            jax.ShapeDtypeStruct((padded, LANES), jnp.int32),
            jax.ShapeDtypeStruct((8, LANES), jnp.int32),
        ),
        in_specs=[smem, vmem, vmem],
        out_specs=(vmem, vmem),
        compiler_params=settings(BIG),
    )(me.astype(jnp.int32).reshape(1), x_cols.T, p_cols.T)
    largest = lax.pmax(largest[0, 0], "groups")

    lists = pltpu.SMEM((2, 32), jnp.int32)
    table = pltpu.SMEM((padded, LANES), jnp.int32)
    remaining = most - first
    inner, up, down = pl.pallas_call(
        partial(inner_kernel, dims, scale),
        out_shape=[
            shaped((rows - 2 * BAND) * pnz), shaped(first), shaped(first)
        ],
        in_specs=[hbm, hbm],
        out_specs=[hbm] * 3,
        scratch_shapes=[
            table,
            scratch(padded * nnz + 1),
            scratch((rows - 2 * BAND) * pnz),
            lists,
            pltpu.SemaphoreType.DMA((1,)),
            pltpu.SemaphoreType.DMA((1,)),
            pltpu.SemaphoreType.DMA((2, first)),
        ],
        compiler_params=settings(BIG),
        cost_estimate=cost((rows - 2 * BAND) * nnz * pnz, 200),
    )(ints, x)
    far_low = lax.ppermute(up, AXES, forward)
    far_high = lax.ppermute(down, AXES, backward)

    half_edge = BAND * pnz
    lefts_count = sum(span[2] for span in crossing(dims, False)[:BAND])

    def half_of_rows(upper, near_rows, *made):
        return pl.pallas_call(
            partial(near_kernel, dims, scale, upper),
            out_shape=[
                shaped(rows * pnz), shaped(half_edge, jnp.float32),
                shaped(half_edge, jnp.float32),
                shaped(remaining),
                shaped(lefts_count),
            ],
            in_specs=[hbm] * (4 + len(made)),
            out_specs=[hbm] * 5,
            input_output_aliases={4: 0} if made else {},
            scratch_shapes=[
                table,
                scratch(padded * nnz + 1),
                scratch(rows * pnz + 1),
                scratch((rows // 2 - BAND) * pnz),
                scratch(half_edge, jnp.float32),
                scratch(half_edge, jnp.float32),
                pltpu.SMEM((32,), jnp.int32),
                pltpu.SemaphoreType.DMA((1,)),
                pltpu.SemaphoreType.DMA((3,)),
                pltpu.SemaphoreType.DMA((remaining,)),
                pltpu.SemaphoreType.DMA((BAND,)),
            ],
            compiler_params=settings(BIG),
            cost_estimate=cost((2 * BAND + rows // 2) * nnz * pnz, 500),
        )(ints, x, near_rows, inner, *made)

    out, part_low, gram_low, down_rest, left_low = half_of_rows(False, low)
    out, part_high, gram_high, up_rest, left_high = half_of_rows(True, high, out)

    def send_rest(state):
        _, up, down = state
        return False, lax.ppermute(up, AXES, forward), lax.ppermute(down, AXES, backward)

    _, more_low, more_high = lax.while_loop(
        lambda state: state[0], send_rest, (largest > first, up_rest, down_rest)
    )

    operands = [
        ints, x, left_low, left_high, far_low, far_high, more_low, more_high, gram_low, gram_high, part_low,
        part_high, out,
    ]
    out = pl.pallas_call(
        partial(far_kernel, dims, scale),
        out_shape=shaped(rows * pnz),
        in_specs=[hbm] * len(operands),
        out_specs=hbm,
        input_output_aliases={len(operands) - 1: 0},
        scratch_shapes=[
            table,
            scratch(padded * nnz + 1),
            scratch(2 * most + 1),
            scratch(edge + 1),
            scratch(edge, jnp.float32),
            scratch(edge, jnp.float32),
            scratch(edge),
            pltpu.SemaphoreType.DMA((1,)),
            pltpu.SemaphoreType.DMA((14 + 2 * BAND,)),
        ],
        compiler_params=settings(BIG),
        cost_estimate=cost(2 * BAND * nnz * pnz, 400),
    )(*operands)
    return out.reshape(rows, pnz, size, size)


def solution(mesh):
    return jax.shard_map(
        body,
        mesh=mesh,
        in_specs=(
            P(("groups", "grid", "rep"), None, None, None),
            P("groups", None),
            P("groups", None),
        ),
        out_specs=P(("groups", "grid", "rep"), None, None, None),
        check_vma=False,
    )
```

```python
from functools import partial

import jax
import jax.numpy as jnp
from jax import lax
from jax.experimental import pallas as pl
from jax.experimental.pallas import tpu as pltpu
from jax.sharding import PartitionSpec as P

BAND = 4
REACH = 2 * BAND
CENTRE = 3 * BAND
AXES = ("grid", "rep")
MIB = 1024 * 1024
FIRST = 16
BIG = 62
TO_X, TO_GRAM, TO_FAR, TO_HALO = 0, 32, 64, 96
LANES = 128
SPARE = 25
SENT = TO_HALO + SPARE


def shift_lane(s):
    return TO_X + SPARE + s


def want_lane(p):
    free = 32 - SPARE
    return (TO_GRAM + SPARE + p) if p < free else (TO_FAR + SPARE + p - free)


def bit_count(v):
    v = v - ((v >> 1) & 0x55555555)
    v = (v & 0x33333333) + ((v >> 2) & 0x33333333)
    v = (v + (v >> 4)) & 0x0F0F0F0F
    return (v + (v >> 8) + (v >> 16)) & 0x3F


def plan_kernel(dims, me, x_cols, p_cols, ints, largest):
    rows, nnz, pnz = dims
    total = x_cols.shape[1]
    padded = rows + 2 * REACH
    most = BAND * nnz
    edge = 2 * BAND * pnz
    lane = lax.broadcasted_iota(jnp.int32, (8, total), 1)
    sub = lax.broadcasted_iota(jnp.int32, (8, total), 0)

    def offsets(ref, count, reach):
        index = lax.broadcasted_iota(jnp.int32, (count, total), 1)
        off = ref[...] - index
        off = jnp.where(off < -reach, off + total, off)
        return jnp.where(off > reach, off - total, off)

    x_off, p_off = offsets(x_cols, nnz, BAND), offsets(p_cols, pnz, REACH)

    def masks(off, reach, axis):
        one = jnp.int32(1)
        parts = [
            lax.slice_in_dim(off, s, s + 1, axis=axis) for s in range(off.shape[axis])
        ]
        return sum(one << (part + reach) for part in parts)

    x_mask = jnp.broadcast_to(masks(x_off, BAND, 0), (8, total))
    p_mask = jnp.broadcast_to(masks(p_off, REACH, 0), (8, total))

    def framed(mask, t, left):
        return pltpu.roll(mask, (REACH - t) % total, 1) << left

    x_frame = [framed(x_mask, t, t) for t in range(2 * REACH)]
    p_frame = {t: framed(p_mask, t, t - BAND) for t in range(BAND, 3 * BAND)}

    def holds(mask, t):
        return -((mask >> (t + BAND)) & 1)

    def side(i, k, far):
        wanted = {}
        for tk in range(k, k + BAND):
            found = jnp.zeros_like(x_mask)
            for ti in range(i, i + BAND):
                found = found | (p_frame[ti] & holds(x_frame[ti], tk))
            wanted[tk] = found & p_frame[tk]
        used = []
        for tf in range(far, far + BAND):
            found = jnp.zeros_like(x_mask)
            for tk in range(k, k + BAND):
                found = found | (wanted[tk] & holds(x_frame[tk], tf))
            used.append((found & x_frame[tf]) >> tf)
        return used

    up, down = side(REACH, BAND, 0), side(BAND, REACH, 3 * BAND)
    needed = jnp.maximum(sum(map(bit_count, up)), sum(map(bit_count, down)))
    needed = jnp.where(lane % rows == 0, needed, 0)
    largest[...] = jnp.broadcast_to(jnp.max(needed, axis=(0, 1), keepdims=True), largest.shape)

    used = jnp.zeros_like(x_mask)
    for q, mask in enumerate(up + down):
        used = jnp.where(sub == q, mask, used)
    here = me[0] * rows
    above = jnp.where(here + rows == total, 0, here + rows)
    at_here = jnp.sum(jnp.where(lane == here, used, 0), axis=1, keepdims=True)
    at_above = jnp.sum(jnp.where(lane == above, used, 0), axis=1, keepdims=True)

    def one(column, q):
        return lax.slice_in_dim(column, q, q + 1, axis=0)

    row = lax.broadcasted_iota(jnp.int32, (padded, 1), 0)
    wide_lane = lax.broadcasted_iota(jnp.int32, (padded, total), 1)
    wide_row = lax.broadcasted_iota(jnp.int32, (padded, total), 0)
    source = here - REACH + wide_row
    source = jnp.where(source < 0, source + total, source)
    source = jnp.where(source >= total, source - total, source)
    pick = (wide_lane == source).astype(jnp.float32)

    def picked(off):
        return lax.dot_general(
            pick, off.astype(jnp.float32), (((1,), (1,)), ((), ())),
            preferred_element_type=jnp.float32,
        ).astype(jnp.int32)

    dx, dp = picked(x_off), picked(p_off)
    x_row, p_row = masks(dx, BAND, 1), masks(dp, REACH, 1)
    far_row = jnp.zeros((padded, 1), jnp.int32)
    far_base = jnp.zeros((padded, 1), jnp.int32)
    sent = jnp.zeros((padded, 1), jnp.int32)
    base_low = jnp.zeros((1, 1), jnp.int32)
    base_high = jnp.full((1, 1), most, jnp.int32)
    for q in range(BAND):
        t = BAND - 1 - q
        low, high = one(at_here, t), one(at_above, BAND + q)
        place = padded - BAND + q
        far_row = jnp.where(row == t, low, jnp.where(row == place, high, far_row))
        far_base = jnp.where(row == t, base_low, jnp.where(row == place, base_high, far_base))
        base_low = base_low + bit_count(low)
        base_high = base_high + bit_count(high)
        sent = jnp.where(row == rows + t, one(at_above, t), sent)
        sent = jnp.where(row == REACH + BAND + q, one(at_here, BAND + q), sent)

    column = lax.broadcasted_iota(jnp.int32, (padded, LANES), 1)
    place = column & 31

    def looked_up(mask, reach):
        at = place - (CENTRE - reach)
        inside = (at >= 0) & (at <= 2 * reach)
        at = jnp.where(inside, at, 0)
        return inside & (((mask >> at) & 1) == 1), bit_count(mask & ((1 << at) - 1))

    close = (row >= BAND) & (row < padded - BAND)
    own = (row >= REACH) & (row < REACH + rows)
    x_hit, x_slot = looked_up(x_row, BAND)
    p_hit, p_slot = looked_up(p_row, REACH)
    far_hit, far_rank = looked_up(far_row, BAND)
    halo = jnp.where(row < REACH, row - BAND, row - rows - REACH + BAND) * pnz
    table = jnp.where(x_hit & close, row * nnz + x_slot, padded * nnz)
    to_gram = jnp.where(p_hit & own, (row - REACH) * pnz + p_slot, rows * pnz)
    to_far = jnp.where(far_hit, far_base + far_rank, 2 * most)
    to_halo = jnp.where(p_hit & close & ~own, halo + p_slot, edge)
    table = jnp.where(column >= TO_GRAM, to_gram, table)
    table = jnp.where(column >= TO_FAR, to_far, table)
    table = jnp.where(column >= TO_HALO, to_halo, table)
    for s in range(nnz):
        table = jnp.where(column == shift_lane(s), lax.slice_in_dim(dx, s, s + 1, axis=1), table)
    for p in range(pnz):
        table = jnp.where(column == want_lane(p), lax.slice_in_dim(dp, p, p + 1, axis=1), table)
    ints[...] = jnp.where(column == SENT, sent, table)


def products(dims, ints, r, slots, table, left, right, base=0):
    _, nnz, pnz = dims
    shift = {s: ints[r, shift_lane(s)] for s in slots}
    want = [ints[r, want_lane(p)] + CENTRE for p in range(pnz)]
    own = jnp.concatenate([left[r * nnz + s - base] for s in slots], axis=1)
    size = left.shape[1]
    blocks = []
    for p in range(0, pnz, 2):
        columns = [
            jnp.concatenate(
                [right[ints[r + shift[s], table + want[q] - shift[s]]] for s in slots], axis=0
            )
            for q in (p, p + 1)
        ]
        pair = jnp.dot(
            own, jnp.concatenate(columns, axis=1), preferred_element_type=jnp.float32
        )
        blocks += [pair[:, :size], pair[:, size:]]
    return blocks


def clear(ref):
    ref[ref.shape[0] - 1] = jnp.zeros(ref.shape[1:], ref.dtype)


def begin(sems, moves):
    copies = []
    for n, (source, target, place) in enumerate(moves):
        copy = pltpu.make_async_copy(
            source, target.at[pl.ds(place, source.shape[0])], sems.at[n]
        )
        copy.start()
        copies.append(copy)
    return copies


def table_copy(source, ints, sem):
    copy = pltpu.make_async_copy(source, ints, sem.at[0])
    copy.start()
    return copy


def finish(copies):
    for copy in copies:
        copy.wait()


def gather(dims, ints, side, skip, pool, out, picks, sem):
    rows, nnz, _ = dims
    top = REACH + rows - BAND - 1
    rows_sent = [top - q if side == 0 else REACH + BAND + q for q in range(BAND)]
    for n in range(skip + out.shape[0]):
        picks[n] = rows_sent[0] * nnz
    count = jnp.int32(0)
    for r in rows_sent:
        for s in range(nnz):
            picks[count] = r * nnz + s
            count = count + ((ints[r, SENT] >> (ints[r, shift_lane(s)] + BAND)) & 1)
    copies = []
    for n in range(out.shape[0]):
        copy = pltpu.make_async_copy(
            pool.at[pl.ds(picks[skip + n], 1)], out.at[pl.ds(n, 1)], sem.at[n]
        )
        copy.start()
        copies.append(copy)
    return copies


def in_pairs(count, step):
    @pl.loop(0, count // 2)
    def _(half):
        step(2 * half)
        step(2 * half + 1)


def gram_row(dims, scale, ints, i, pool, gram, place):
    pnz = dims[2]
    blocks = products(dims, ints, REACH + i, range(dims[1]), TO_X, pool, pool)
    for p, block in enumerate(blocks):
        gram[place * pnz + p] = (block * scale).astype(gram.dtype)


def update_row(dims, ints, i, pool, gram, target, place):
    pnz = dims[2]
    r = REACH + i
    blocks = products(dims, ints, r, range(dims[1]), TO_GRAM, pool, gram)
    for p, block in enumerate(blocks):
        kept = pool[ints[r, TO_X + ints[r, want_lane(p)] + CENTRE]].astype(jnp.float32)
        target[place * pnz + p] = (1.5 * kept - 0.5 * block).astype(target.dtype)


def crossing(dims, upper):
    rows, nnz, _ = dims
    if upper:
        spans = [(nnz - 1 - e, e + 1) for e in range(BAND)]
        listed = [rows + e for e in range(BAND)] + [rows - BAND + e for e in range(BAND)]
    else:
        spans = [(0, BAND - e) for e in range(BAND)]
        listed = [e - BAND for e in range(BAND)] + list(range(BAND))
    return [(row, *span) for row, span in zip(listed, spans + spans)]


def inner_kernel(
    dims, scale, table, x, out, up, down, ints, pool, gram, picks, table_sem, sems, pick_sems
):
    rows, nnz, pnz = dims
    copies = [table_copy(table, ints, table_sem)] + begin(sems, [(x, pool, REACH * nnz)])
    clear(pool)
    finish(copies)
    listed = []
    for side, sent in enumerate((up, down)):
        listed += gather(dims, ints, side, 0, pool, sent, picks.at[side], pick_sems.at[side])
    in_pairs(rows - 2 * BAND, lambda n: gram_row(dims, scale, ints, BAND + n, pool, gram, n))
    finish(begin(sems, [(gram, out, 0)]) + listed)


def near_kernel(dims, scale, upper, table, x, near, inner, *rest):
    out, part, gram_part, sent, lefts, ints, *scratch = rest[-16:]
    pool, gram, done, own_sums, near_sums, picks, table_sem, sems, pick_sems, left_sems = scratch
    rows, nnz, pnz = dims
    half, many = rows // 2, near.shape[0]
    start = REACH * nnz
    mine = half * nnz
    x_from = mine if upper else 0
    near_at = start + 2 * mine if upper else start - many
    copies = [table_copy(table, ints, table_sem)] + begin(sems, [
        (near, pool, near_at), (x.at[pl.ds(x_from, mine)], pool, start + x_from),
        (inner, gram, BAND * pnz),
    ])
    clear(pool)
    clear(gram)
    edge = rows - BAND if upper else 0
    halo = rows if upper else -BAND
    full = half if upper else BAND

    def halo_row(n):
        blocks = products(dims, ints, REACH + halo + n, range(nnz), TO_X, pool, pool)
        for p, block in enumerate(blocks):
            near_sums[n * pnz + p] = block.astype(near_sums.dtype)

    def edge_row(n):
        blocks = products(dims, ints, REACH + edge + n, range(nnz), TO_GRAM, pool, gram)
        for p, block in enumerate(blocks):
            own_sums[n * pnz + p] = block.astype(own_sums.dtype)

    finish(copies[:3])
    side, skip = 0 if upper else 1, BAND * nnz - sent.shape[0]
    laid = gather(dims, ints, side, skip, pool, sent, picks, pick_sems)
    place, moves = 0, []
    for row, slot, count in crossing(dims, upper)[:BAND]:
        moves.append((pool.at[pl.ds((REACH + row) * nnz + slot, count)], lefts, place))
        place += count
    laid += begin(left_sems, moves)
    in_pairs(BAND, halo_row)
    first = begin(sems.at[pl.ds(0, 1)], [(near_sums, gram_part, 0)])
    finish(copies[3:])
    in_pairs(BAND, lambda n: gram_row(dims, scale, ints, edge + n, pool, gram, edge + n))
    in_pairs(BAND, edge_row)
    second = begin(sems.at[pl.ds(1, 1)], [(own_sums, part, 0)])
    in_pairs(half - BAND, lambda n: update_row(dims, ints, full + n, pool, gram, done, n))
    third = begin(sems.at[pl.ds(2, 1)], [(done, out, full * pnz)])
    finish(first + second + third + laid)


def far_kernel(
    dims, scale, table, x, left_low, left_high, far_low, far_high, more_low, more_high, gram_low, gram_high,
    part_low, part_high, unused, out, ints, pool, left, far, gram, near_sums, own_sums, done, table_sem,
    sems
):
    rows, nnz, pnz = dims
    first, near, own = far_low.shape[0], BAND * nnz, x.shape[0]
    edge = BAND * pnz
    start = REACH * nnz
    moves = [
        (far_low, far, 0), (more_low, far, first),
        (far_high, far, near), (more_high, far, near + first),
    ]
    moves += [(left_low, left, 0), (left_high, left, left_low.shape[0])]
    early = [table_copy(table, ints, table_sem)] + begin(sems, moves)
    late = begin(sems.at[pl.ds(len(moves), 6)], [
        (gram_low, near_sums, 0), (gram_high, near_sums, edge),
        (x.at[pl.ds(0, near)], pool, start), (part_low, own_sums, 0),
        (x.at[pl.ds(own - near, near)], pool, start + own - near), (part_high, own_sums, edge),
    ])
    used = len(moves) + len(late)
    clear(pool)
    clear(far)
    clear(gram)
    finish(early)

    def far_terms(upper):
        place = left_low.shape[0] if upper else 0
        for e, (row, slot, many) in enumerate(crossing(dims, upper)[:BAND]):
            slots = range(slot, slot + many)
            base = (REACH + row) * nnz + slot - place
            place += many
            blocks = products(dims, ints, REACH + row, slots, TO_FAR, left, far, base)
            for p, block in enumerate(blocks):
                n = (upper * BAND + e) * pnz + p
                whole = near_sums[n].astype(jnp.float32) + block
                gram[n] = (whole * scale).astype(gram.dtype)

    def halo_terms(upper, places):
        for e in places:
            row, slot, many = crossing(dims, upper)[BAND + e]
            r = REACH + row
            slots = range(slot, slot + many)
            blocks = products(dims, ints, r, slots, TO_HALO, pool, gram)
            for p, block in enumerate(blocks):
                n = (upper * BAND + e) * pnz + p
                kept = pool[ints[r, TO_X + ints[r, want_lane(p)] + CENTRE]].astype(jnp.float32)
                whole = own_sums[n].astype(jnp.float32) + block
                done[n] = (1.5 * kept - 0.5 * whole).astype(done.dtype)
        at, many = (upper * BAND + places[0]) * pnz, len(places) * pnz
        place = (places[0] + (rows - BAND if upper else 0)) * pnz
        return begin(
            sems.at[pl.ds(used + 2 * upper + places[0] // 2, 1)],
            [(done.at[pl.ds(at, many)], out, place)],
        )

    finish(late[:1])
    far_terms(False)
    finish(late[1:2])
    far_terms(True)
    finish(late[2:4])
    half = BAND // 2
    outgoing = halo_terms(False, range(BAND))
    finish(late[4:])
    outgoing += halo_terms(True, range(half, BAND))
    outgoing += halo_terms(True, range(half))
    finish(outgoing)


def body(x_vals, x_cols, p_cols):
    rows, nnz, size, _ = x_vals.shape
    pnz = p_cols.shape[1]
    count = lax.axis_size(AXES)
    me = lax.axis_index(AXES)
    first_row = me * rows
    scale = 1.0 / (4 * nnz * size)
    padded = rows + 2 * REACH
    forward = [(i, (i + 1) % count) for i in range(count)]
    backward = [(target, source) for source, target in forward]
    near = BAND * nnz
    edge = 2 * BAND * pnz
    most = near
    first = min(FIRST, most)
    product = 2 * size ** 3
    block = (size, size)

    smem = pl.BlockSpec(memory_space=pltpu.SMEM)
    hbm = pl.BlockSpec(memory_space=pl.ANY)
    vmem = pl.BlockSpec(memory_space=pltpu.VMEM)

    def shaped(blocks, kind=jnp.bfloat16):
        return jax.ShapeDtypeStruct((blocks,) + block, kind)

    def scratch(blocks, kind=jnp.bfloat16):
        return pltpu.VMEM((blocks,) + block, kind)

    def settings(mib):
        return pltpu.CompilerParams(vmem_limit_bytes=mib * MIB)

    def cost(products_made, blocks_moved):
        return pl.CostEstimate(
            flops=products_made * product, bytes_accessed=blocks_moved * 2 * size * size,
            transcendentals=0,
        )

    x = x_vals.reshape(rows * nnz, size, size)
    low = lax.ppermute(x[rows * nnz - near:], AXES, forward)
    high = lax.ppermute(x[:near], AXES, backward)

    dims = (rows, nnz, pnz)
    ints, largest = pl.pallas_call(
        partial(plan_kernel, dims),
        out_shape=(
            jax.ShapeDtypeStruct((padded, LANES), jnp.int32),
            jax.ShapeDtypeStruct((8, LANES), jnp.int32),
        ),
        in_specs=[smem, vmem, vmem],
        out_specs=(vmem, vmem),
        compiler_params=settings(BIG),
    )(me.astype(jnp.int32).reshape(1), x_cols.T, p_cols.T)
    largest = lax.pmax(largest[0, 0], "groups")

    lists = pltpu.SMEM((2, 32), jnp.int32)
    table = pltpu.SMEM((padded, LANES), jnp.int32)
    remaining = most - first
    inner, up, down = pl.pallas_call(
        partial(inner_kernel, dims, scale),
        out_shape=[
            shaped((rows - 2 * BAND) * pnz), shaped(first), shaped(first)
        ],
        in_specs=[hbm, hbm],
        out_specs=[hbm] * 3,
        scratch_shapes=[
            table,
            scratch(padded * nnz + 1),
            scratch((rows - 2 * BAND) * pnz),
            lists,
            pltpu.SemaphoreType.DMA((1,)),
            pltpu.SemaphoreType.DMA((1,)),
            pltpu.SemaphoreType.DMA((2, first)),
        ],
        compiler_params=settings(BIG),
        cost_estimate=cost((rows - 2 * BAND) * nnz * pnz, 200),
    )(ints, x)
    far_low = lax.ppermute(up, AXES, forward)
    far_high = lax.ppermute(down, AXES, backward)

    half_edge = BAND * pnz
    lefts_count = sum(span[2] for span in crossing(dims, False)[:BAND])

    def half_of_rows(upper, near_rows, *made):
        return pl.pallas_call(
            partial(near_kernel, dims, scale, upper),
            out_shape=[
                shaped(rows * pnz), shaped(half_edge, jnp.float32),
                shaped(half_edge, jnp.float32),
                shaped(remaining),
                shaped(lefts_count),
            ],
            in_specs=[hbm] * (4 + len(made)),
            out_specs=[hbm] * 5,
            input_output_aliases={4: 0} if made else {},
            scratch_shapes=[
                table,
                scratch(padded * nnz + 1),
                scratch(rows * pnz + 1),
                scratch((rows // 2 - BAND) * pnz),
                scratch(half_edge, jnp.float32),
                scratch(half_edge, jnp.float32),
                pltpu.SMEM((32,), jnp.int32),
                pltpu.SemaphoreType.DMA((1,)),
                pltpu.SemaphoreType.DMA((3,)),
                pltpu.SemaphoreType.DMA((remaining,)),
                pltpu.SemaphoreType.DMA((BAND,)),
            ],
            compiler_params=settings(BIG),
            cost_estimate=cost((2 * BAND + rows // 2) * nnz * pnz, 500),
        )(ints, x, near_rows, inner, *made)

    out, part_low, gram_low, down_rest, left_low = half_of_rows(False, low)
    out, part_high, gram_high, up_rest, left_high = half_of_rows(True, high, out)

    def send_rest(state):
        _, up, down = state
        return False, lax.ppermute(up, AXES, forward), lax.ppermute(down, AXES, backward)

    _, more_low, more_high = lax.while_loop(
        lambda state: state[0], send_rest, (largest > first, up_rest, down_rest)
    )

    operands = [
        ints, x, left_low, left_high, far_low, far_high, more_low, more_high, gram_low, gram_high, part_low,
        part_high, out,
    ]
    out = pl.pallas_call(
        partial(far_kernel, dims, scale),
        out_shape=shaped(rows * pnz),
        in_specs=[hbm] * len(operands),
        out_specs=hbm,
        input_output_aliases={len(operands) - 1: 0},
        scratch_shapes=[
            table,
            scratch(padded * nnz + 1),
            scratch(2 * lefts_count),
            scratch(2 * most + 1),
            scratch(edge + 1),
            scratch(edge, jnp.float32),
            scratch(edge, jnp.float32),
            scratch(edge),
            pltpu.SemaphoreType.DMA((1,)),
            pltpu.SemaphoreType.DMA((14 + 2 * BAND,)),
        ],
        compiler_params=settings(BIG),
        cost_estimate=cost(2 * BAND * nnz * pnz, 400),
    )(*operands)
    return out.reshape(rows, pnz, size, size)


def solution(mesh):
    return jax.shard_map(
        body,
        mesh=mesh,
        in_specs=(
            P(("groups", "grid", "rep"), None, None, None),
            P("groups", None),
            P("groups", None),
        ),
        out_specs=P(("groups", "grid", "rep"), None, None, None),
        check_vma=False,
    )
```
